32 devices in a mesh: seq: 2 (over y), fsdp: 16 (over z, x, core).
Axes of the slice: x: 2, y: 2, z: 4, core: 2. Of those that a mesh axis runs over, the one named last changes fastest.
Arguments:
- tokens: bfloat16 [16, 512, 2048], P('fsdp', 'seq'), may hold values from -6 to 6
- bounds: int32 [4], replicated, may hold values from 1 to 2047, as said below
- norm_attn: bfloat16 [2048], P('fsdp'), may hold values from 0.099609375 to 1.8984375
- weight_qkv: bfloat16 [2048, 6144], P('fsdp'), may hold values from -0.125 to 0.125
- weight_out: bfloat16 [2048, 2048], P('fsdp'), may hold values from -2 to 2
- norm_ffn: bfloat16 [2048], P('fsdp'), may hold values from 0.099609375 to 1.8984375
- weight_gate: bfloat16 [2048, 5504], P('fsdp'), may hold values from -0.125 to 0.125
- weight_up: bfloat16 [2048, 5504], P('fsdp'), may hold values from -0.125 to 0.125
- weight_down: bfloat16 [5504, 2048], P('fsdp'), may hold values from -0.078125 to 0.078125
- cotangent: bfloat16 [16, 512, 2048], P('fsdp', 'seq'), may hold values from -6 to 6
Outputs:
- block_out: bfloat16 [16, 512, 2048], P('fsdp', 'seq')
- grad_tokens: float32 [16, 512, 2048], P('fsdp', 'seq')
- grad_norm_attn: float32 [2048], P('fsdp')
- grad_qkv: float32 [2048, 6144], P('fsdp')
- grad_out: float32 [2048, 2048], P('fsdp')
- grad_norm_ffn: float32 [2048], P('fsdp')
- grad_gate: float32 [2048, 5504], P('fsdp')
- grad_up: float32 [2048, 5504], P('fsdp')
- grad_down: float32 [5504, 2048], P('fsdp')
The draws below stay inside these ranges and needn't reach their ends.
Inputs may be any that keep to these rules, and one draw needn't show every extreme that they name: Sequence i holds two documents, its tokens before position bounds[i] and those from it on; both ends of the range occur in every draw.
All inputs are finite; a program needn't handle non-finite values.
Results may differ from the reference program's by a relative error of at most 0.02.
Values may be sent and summed in bfloat16 or wider, within the bound.
No kernel may reach another device: no remote copies, remote signals or barrier semaphores. Data moves between devices by JAX's collectives and lax.ppermute only.
A program may use at most 576 MiB of HBM per device.

```python
import jax
import jax.numpy as jnp
from jax import lax

D = 2048
H = 16
HD = 128
FF = 5504
WINDOW = 1024
RUN = 512
SEQ_LEN = 2048
SEQS = 4
RUNS = 16


def draw_bounds(key, part):
    key_one, key_three, key_four = jax.random.split(key, 3)
    values = jax.random.randint(key_one, (SEQS,), 1, SEQ_LEN)
    low_spot = jax.random.randint(key_three, (), 0, SEQS)
    high_spot = (low_spot + 1 + jax.random.randint(key_four, (), 0, SEQS - 1)) % SEQS
    values = values.at[low_spot].set(1)
    values = values.at[high_spot].set(SEQ_LEN - 1)
    return values.astype(jnp.int32)


def spiked(entries, rng, source, target, parts, factor):
    owner, partner = [(jnp.arange(entries.shape[axis_at]) // (entries.shape[axis_at] // parts)).reshape([-1 if axis == axis_at else 1 for axis in range(entries.ndim)]) for axis_at in (source, target)]
    chosen = jax.random.permutation(rng, parts)[partner]
    strong = (owner == chosen) | (owner == (partner + parts // 2) % parts)
    return jnp.where(strong, factor * entries, entries)


def block_levels(key, shape, cuts, low, top_value):
    level = 1.0
    for position, parts in cuts:
        draws = jax.random.uniform(jax.random.fold_in(jax.random.fold_in(key, 6), position), (parts,), jnp.float32, low / len(cuts), top_value / len(cuts))
        level = level * jnp.repeat(jnp.exp(draws), shape[position] // parts).reshape((-1,) + (1,) * (len(shape) - 1 - position))
    return level


def normal_values(stream_key, extent, deviation, bound, cuts=(), kind=jnp.bfloat16):
    values = deviation * jax.random.normal(stream_key, extent, jnp.float32)
    if cuts:
        values = values * block_levels(stream_key, extent, cuts, -0.22, 0.18)
    return jnp.clip(values, -bound, bound).astype(kind)


def heavy_noise(own_key, shape, scale, limit, shards, heavy, held_as=jnp.bfloat16):
    array = scale * jax.random.normal(own_key, shape, jnp.float32)
    if shards:
        array = array * block_levels(own_key, shape, shards, -0.22, 0.18)
    return jnp.clip(spiked(array, jax.random.fold_in(own_key, 3), *heavy), -limit, limit).astype(held_as)


def setup_inputs(seed: int = 0) -> dict:
    seeds = jax.random.split(jax.random.key(seed), 11)
    tokens = normal_values(seeds[0], (RUNS, RUN, D), 1.0, 6.0, ((0, 16), (1, 2)))
    bounds = draw_bounds(jax.random.fold_in(seeds[10], 71), 0)
    norm_attn = jnp.clip(1.0 + 0.18 * jax.random.normal(seeds[2], (D,), jnp.float32), 0.099609375, 1.8984375).astype(jnp.bfloat16)
    weight_qkv = normal_values(seeds[3], (D, 3 * D), D ** -0.5, 0.125, ((0, 16),))
    weight_out = normal_values(seeds[4], (D, D), (max(4 * D // WINDOW, 1)) ** -0.5, 2.0, ((0, 16),))
    norm_ffn = jnp.clip(1.0 + 0.18 * jax.random.normal(seeds[5], (D,), jnp.float32), 0.099609375, 1.8984375).astype(jnp.bfloat16)
    weight_gate = normal_values(seeds[6], (D, FF), D ** -0.5, 0.125, ((0, 16),))
    weight_up = normal_values(seeds[7], (D, FF), D ** -0.5, 0.125, ((0, 16),))
    weight_down = normal_values(seeds[8], (FF, D), FF ** -0.5, 0.078125, ((0, 16),))
    cotangent = heavy_noise(seeds[9], (RUNS, RUN, D), 1.0, 6.0, ((0, 16), (1, 2)), (0, 2, 16, 2.0))
    return {"tokens": tokens, "bounds": bounds, "norm_attn": norm_attn, "weight_qkv": weight_qkv, "weight_out": weight_out, "norm_ffn": norm_ffn, "weight_gate": weight_gate, "weight_up": weight_up, "weight_down": weight_down, "cotangent": cotangent}


EPS = 1e-05
NEG = -1e+30
THETA = 10000.0
HIGH = lax.Precision.HIGHEST

@jax.custom_vjp
def low(v):
    return lax.optimization_barrier(v.astype(jnp.bfloat16)).astype(jnp.float32)

@jax.custom_vjp
def low_back(v):
    return v

def low_keep(v):
    return (low(v), None)

def low_pass(kept, grad):
    return (grad,)

def back_keep(v):
    return (v, None)

def back_low(kept, grad):
    return (low(grad),)
low.defvjp(low_keep, low_pass)
low_back.defvjp(back_keep, back_low)

def rms_norm(values, gain):
    scale_row = lax.rsqrt(lax.optimization_barrier(jnp.mean(values * values, axis=-1, keepdims=True)) + EPS)
    return values * scale_row * gain

def rope_tables(length, head_size):
    positions = jnp.arange(length, dtype=jnp.float32)
    frequency = THETA ** (-jnp.arange(head_size // 2, dtype=jnp.float32) * 2.0 / head_size)
    angles = positions[:, None] * frequency[None, :]
    return (jnp.cos(angles)[:, None, :], jnp.sin(angles)[:, None, :])

def rotate(vector, cosine, sine_table):
    half_size = vector.shape[-1] // 2
    front_half = vector[..., :half_size]
    back_half = vector[..., half_size:]
    return jnp.concatenate([front_half * cosine - back_half * sine_table, back_half * cosine + front_half * sine_table], axis=-1)

def block_attend(query_block, block_start, key_rot, value_all, boundary):
    block_rows = query_block.shape[1]
    length = key_rot.shape[1]
    raw_scores = jnp.einsum('bqhd,bkhd->bhqk', query_block, key_rot, precision=HIGH) * HD ** (-0.5)
    scores = low_back(raw_scores)
    query_pos = block_start + jnp.arange(block_rows, dtype=jnp.int32)
    key_pos = jnp.arange(length, dtype=jnp.int32)
    behind = query_pos[:, None] - key_pos[None, :]
    in_window = (behind >= 0) & (behind < WINDOW)
    query_after = query_pos[None, :] >= boundary[:, None]
    key_after = key_pos[None, :] >= boundary[:, None]
    allowed = in_window[None] & (query_after[:, :, None] == key_after[:, None, :])
    scores = jnp.where(allowed[:, None], scores, NEG)
    top_score = lax.optimization_barrier(jnp.max(scores, axis=-1, keepdims=True))
    powered = jnp.exp(scores - top_score)
    prob_low = low(powered / lax.optimization_barrier(jnp.sum(powered, axis=-1, keepdims=True)))
    return jnp.einsum('bhqk,bkhd->bqhd', prob_low, value_all, precision=HIGH)

def layer(inputs, boundary, gain_attn, weight_qkv, weight_out, gain_ffn, weight_gate, weight_up, weight_down):
    batch_size, length, model_width = inputs.shape
    act_attn = low(rms_norm(inputs, gain_attn))
    proj_qkv = low_back(jnp.dot(act_attn, weight_qkv, precision=HIGH)).reshape(batch_size, length, 3, H, HD)
    cosine, sine_table = rope_tables(length, HD)
    query_rot = low(low_back(rotate(proj_qkv[:, :, 0], cosine, sine_table)))
    key_rot = low(low_back(rotate(proj_qkv[:, :, 1], cosine, sine_table)))
    value_all = low(low_back(proj_qkv[:, :, 2]))
    block_rows = min(length, 512)
    block_count = length // block_rows
    query_blocks = query_rot.reshape(batch_size, block_count, block_rows, H, HD).transpose(1, 0, 2, 3, 4)
    block_starts = jnp.arange(block_count, dtype=jnp.int32) * block_rows
    checked = jax.checkpoint(block_attend)

    def one_block(block_item):
        return checked(block_item[0], block_item[1], key_rot, value_all, boundary)
    head_blocks = lax.map(one_block, (query_blocks, block_starts))
    head_out = head_blocks.transpose(1, 0, 2, 3, 4).reshape(batch_size, length, H, HD)
    head_out = low(low_back(head_out)).reshape(batch_size, length, model_width)
    middle = inputs + low_back(jnp.dot(head_out, weight_out, precision=HIGH))
    act_ffn = low(rms_norm(middle, gain_ffn))
    gate_proj = low_back(jnp.dot(act_ffn, weight_gate, precision=HIGH))
    up_proj = low_back(jnp.dot(act_ffn, weight_up, precision=HIGH))
    hidden = low(jax.nn.silu(gate_proj) * up_proj)
    return middle + low_back(jnp.dot(hidden, weight_down, precision=HIGH))

def reference(tokens, bounds, norm_attn, weight_qkv, weight_out, norm_ffn, weight_gate, weight_up, weight_down, cotangent):
    params = (norm_attn.astype(jnp.float32), weight_qkv.astype(jnp.float32), weight_out.astype(jnp.float32), norm_ffn.astype(jnp.float32), weight_gate.astype(jnp.float32), weight_up.astype(jnp.float32), weight_down.astype(jnp.float32))
    per_group = 1
    for candidate in range(1, SEQS + 1):
        if SEQS % candidate == 0 and candidate * SEQ_LEN <= 4096:
            per_group = candidate
    groups = SEQS // per_group
    inputs = tokens.astype(jnp.float32).reshape(groups, per_group, SEQ_LEN, D)
    grads_in = cotangent.astype(jnp.float32).reshape(groups, per_group, SEQ_LEN, D)
    boundary = bounds.reshape(groups, per_group)

    def step(totals, scan_item):
        seq_block, grad_block, bound_block = scan_item

        def forward(values, gain_attn, w_one, w_two, gain_ffn, w_three, w_four, w_five):
            return layer(values, bound_block, gain_attn, w_one, w_two, gain_ffn, w_three, w_four, w_five)
        result, pull_back = jax.vjp(forward, seq_block, params[0], params[1], params[2], params[3], params[4], params[5], params[6])
        pulled = pull_back(grad_block)
        totals = tuple((running + grad_part for running, grad_part in zip(totals, pulled[1:])))
        return (totals, (result, pulled[0]))
    zero_grads = tuple((jnp.zeros_like(weight) for weight in params))
    totals, (results, grad_rows) = lax.scan(step, zero_grads, (inputs, grads_in, boundary))
    block_out = results.reshape(RUNS, RUN, D).astype(jnp.bfloat16)
    grad_tokens = grad_rows.reshape(RUNS, RUN, D)
    return (block_out, grad_tokens, totals[0], totals[1], totals[2], totals[3], totals[4], totals[5], totals[6])
```

```python
import functools

import jax
import jax.numpy as jnp
from jax import lax
from jax.experimental import pallas as pl
from jax.experimental.pallas import tpu as pltpu
from jax.sharding import Mesh, PartitionSpec as P

HD = 128
WINDOW = 1024
EPS = 1e-05
NEG = -1e30
THETA = 10000.0
F32 = jnp.float32
BF16 = jnp.bfloat16
BITS = (("y", 1), ("x", 2), ("c", 4))
NT = (((1,), (1,)), ((), ()))
TN = (((0,), (0,)), ((), ()))


def axes_of(j):
    return tuple(name for name, bit in BITS if j & bit)


def hop(block, j):
    axes = axes_of(j)
    last = 2 ** len(axes) - 1
    return lax.ppermute(block, axes, [(i, last - i) for i in range(last + 1)])


def gather_plane(block):
    parts = {0: block, 1: hop(block, 1), 2: hop(block, 2), 3: hop(block, 3)}
    for j in range(4):
        parts[j + 4] = hop(parts[j], 4)
    return [parts[j] for j in range(8)]


def exchange_plane(blocks):
    return [blocks[0]] + [hop(blocks[j], j) for j in range(1, 8)]


def scatter_plane(near, far):
    rows = near.shape[0] // 4
    total = (near.astype(F32) + hop(far, 4).astype(F32)).reshape(4, rows, -1)
    own = total[0]
    for j in range(1, 4):
        own = own + hop(total[j].astype(BF16), j).astype(F32)
    return own


def ring_of(size):
    odd = [i for i in range(size) if i % 2 == 1]
    even = [i for i in range(size) if i % 2 == 0 and i > 0]
    return [0] + odd + even[::-1]


def ring_place(z, size, back):
    ring = ring_of(size)
    table = [ring[(ring.index(i) - back) % size] for i in range(size)]
    return jnp.asarray(table, jnp.int32)[z]


def ring_hop(block, size):
    ring = ring_of(size)
    return lax.ppermute(block, "z", [(ring[i], ring[(i + 1) % size]) for i in range(size)])


def ring_gather(block, z, size):
    out = jnp.zeros((size,) + block.shape, block.dtype)
    out = lax.dynamic_update_index_in_dim(out, block, z, 0)
    for back in range(1, size):
        block = ring_hop(block, size)
        out = lax.dynamic_update_index_in_dim(out, block, ring_place(z, size, back), 0)
    return out


def ring_scatter(chunks, z, size):
    total = lax.dynamic_index_in_dim(chunks, ring_place(z, size, 1), 0, False)
    for back in range(2, size + 1):
        moved = ring_hop(total.astype(BF16), size).astype(F32)
        total = moved + lax.dynamic_index_in_dim(
            chunks, ring_place(z, size, back), 0, False
        ).astype(F32)
    return total


def absolute(blocks, rank):
    stacked = jnp.stack(blocks)
    return [
        lax.dynamic_index_in_dim(stacked, jnp.bitwise_xor(rank, i), 0, False)
        for i in range(len(blocks))
    ]


def place_of(block):
    return (block & 1) | ((block >> 1) & 1) << 2 | ((block >> 2) & 1) << 1


def lowest_key(block, rows, bound):
    pos = block * rows + lax.broadcasted_iota(jnp.int32, (rows, 1), 0)
    return jnp.maximum(jnp.where(pos >= bound, bound, 0), pos - (WINDOW - 1))


def block_scores(query, key, low, q_block, k_block, rows):
    scores = lax.dot_general(query, key, NT, preferred_element_type=F32) * HD**-0.5
    pos = k_block * rows + lax.broadcasted_iota(jnp.int32, (rows, rows), 1)
    seen = pos >= low
    if q_block == k_block:
        seen = seen & (
            lax.broadcasted_iota(jnp.int32, (rows, rows), 1)
            <= lax.broadcasted_iota(jnp.int32, (rows, rows), 0)
        )
    return jnp.where(seen, scores, NEG)


def key_blocks(q_block, rows):
    return range(max(0, q_block - WINDOW // rows), q_block + 1)


def attend_kernel(rows, info, proj, cosine, sine, qkv, result, lse):
    count = proj.shape[0] // rows
    rank, bound = info[0], info[1]

    @pl.loop(0, count)
    def _(j):
        at = pl.ds(j * rows, rows)
        for part in range(2):
            value = proj[at, part * HD : (part + 1) * HD]
            turned = value * cosine[at, :] + pltpu.roll(value, HD // 2, 1) * sine[at, :]
            qkv[at, part * HD : (part + 1) * HD] = turned.astype(BF16)
        qkv[at, 2 * HD :] = proj[at, 2 * HD :].astype(BF16)

    def start(block):
        return pl.multiple_of(jnp.bitwise_xor(place_of(block), rank) * rows, rows)

    for b in range(count):
        own = pl.ds(start(b), rows)
        query = qkv[own, :HD]
        low = lowest_key(b, rows, bound)
        spots = [(kb, pl.ds(start(kb), rows)) for kb in key_blocks(b, rows)]
        scores = [
            block_scores(query, qkv[at, HD : 2 * HD], low, b, kb, rows) for kb, at in spots
        ]
        top = functools.reduce(jnp.maximum, [jnp.max(s, axis=1, keepdims=True) for s in scores])
        powered = [jnp.exp(s - top) for s in scores]
        total = functools.reduce(jnp.add, [jnp.sum(p, axis=1, keepdims=True) for p in powered])
        inverse = 1.0 / total
        out = functools.reduce(
            jnp.add,
            [
                jnp.dot(
                    (p * inverse).astype(BF16), qkv[at, 2 * HD :], preferred_element_type=F32
                )
                for p, (_, at) in zip(powered, spots)
            ],
        )
        result[own, :] = out.astype(BF16)
        lse[0, own, :] = top + jnp.log(total)


def attend(info, proj, cosine, sine, rows):
    length = proj.shape[0]
    heads = proj.shape[1] // (3 * HD)
    return pl.pallas_call(
        functools.partial(attend_kernel, rows),
        grid_spec=pltpu.PrefetchScalarGridSpec(
            num_scalar_prefetch=1,
            grid=(heads,),
            in_specs=[
                pl.BlockSpec((length, 3 * HD), lambda h, s: (0, h)),
                pl.BlockSpec((length, HD), lambda h, s: (0, 0)),
                pl.BlockSpec((length, HD), lambda h, s: (0, 0)),
            ],
            out_specs=[
                pl.BlockSpec((length, 3 * HD), lambda h, s: (0, h)),
                pl.BlockSpec((length, HD), lambda h, s: (0, h)),
                pl.BlockSpec((1, length, 1), lambda h, s: (h, 0, 0)),
            ],
        ),
        out_shape=[
            jax.ShapeDtypeStruct(proj.shape, BF16),
            jax.ShapeDtypeStruct((length, heads * HD), BF16),
            jax.ShapeDtypeStruct((heads, length, 1), F32),
        ],
        compiler_params=pltpu.CompilerParams(vmem_limit_bytes=48 * 2**20),
        name="attend",
    )(info, proj, cosine, sine)


def attend_back_kernel(rows, info, qkv, grad, lse, cosine, sine, out, sum_key, sum_value):
    count = qkv.shape[0] // rows
    rank, bound = info[0], info[1]
    sum_key[...] = jnp.zeros_like(sum_key)
    sum_value[...] = jnp.zeros_like(sum_value)

    def start(block):
        return pl.multiple_of(jnp.bitwise_xor(place_of(block), rank) * rows, rows)

    def unturn(value, at):
        value = value.astype(BF16).astype(F32)
        turned = value * cosine[at, :] - pltpu.roll(value, HD // 2, 1) * sine[at, :]
        return turned.astype(BF16)

    for b in range(count):
        own = pl.ds(start(b), rows)
        query = qkv[own, :HD]
        top = grad[own, :]
        low = lowest_key(b, rows, bound)
        log_total = lse[0, own, :]
        spots = [(kb, pl.ds(start(kb), rows)) for kb in key_blocks(b, rows)]
        probs = [
            jnp.exp(block_scores(query, qkv[at, HD : 2 * HD], low, b, kb, rows) - log_total)
            for kb, at in spots
        ]
        grads = [
            lax.dot_general(top, qkv[at, 2 * HD :], NT, preferred_element_type=F32)
            for _, at in spots
        ]
        mean = functools.reduce(
            jnp.add,
            [jnp.sum(p * g, axis=1, keepdims=True) for p, g in zip(probs, grads)],
        )
        sum_query = jnp.zeros((rows, HD), F32)
        for p, g, (_, at) in zip(probs, grads, spots):
            low_grad = (p * (g - mean)).astype(BF16)
            sum_query = sum_query + jnp.dot(
                low_grad, qkv[at, HD : 2 * HD], preferred_element_type=F32
            )
            sum_key[at, :] += lax.dot_general(low_grad, query, TN, preferred_element_type=F32)
            sum_value[at, :] += lax.dot_general(
                p.astype(BF16), top, TN, preferred_element_type=F32
            )
        out[own, :HD] = unturn(sum_query * HD**-0.5, own)

    @pl.loop(0, count)
    def _(j):
        at = pl.ds(pl.multiple_of(j * rows, rows), rows)
        out[at, HD : 2 * HD] = unturn(sum_key[at, :] * HD**-0.5, at)
        out[at, 2 * HD :] = sum_value[at, :].astype(BF16)


def attend_back(info, qkv, grad, lse, cosine, sine, rows):
    length = qkv.shape[0]
    heads = qkv.shape[1] // (3 * HD)
    return pl.pallas_call(
        functools.partial(attend_back_kernel, rows),
        grid_spec=pltpu.PrefetchScalarGridSpec(
            num_scalar_prefetch=1,
            grid=(heads,),
            in_specs=[
                pl.BlockSpec((length, 3 * HD), lambda h, s: (0, h)),
                pl.BlockSpec((length, HD), lambda h, s: (0, h)),
                pl.BlockSpec((1, length, 1), lambda h, s: (h, 0, 0)),
                pl.BlockSpec((length, HD), lambda h, s: (0, 0)),
                pl.BlockSpec((length, HD), lambda h, s: (0, 0)),
            ],
            out_specs=pl.BlockSpec((length, 3 * HD), lambda h, s: (0, h)),
            scratch_shapes=[pltpu.VMEM((length, HD), F32), pltpu.VMEM((length, HD), F32)],
        ),
        out_shape=jax.ShapeDtypeStruct(qkv.shape, BF16),
        compiler_params=pltpu.CompilerParams(vmem_limit_bytes=48 * 2**20),
        name="attend_back",
    )(info, qkv, grad, lse, cosine, sine)


def on_device(
    sizes,
    tokens,
    bounds,
    norm_attn,
    weight_qkv,
    weight_out,
    norm_ffn,
    weight_gate,
    weight_up,
    weight_down,
    cotangent,
):
    planes, shards = sizes
    rows, width = tokens.shape[1], tokens.shape[2]
    hidden_width = weight_gate.shape[1]
    own_rows = weight_qkv.shape[0]
    piece = width // 8
    half_down = weight_down.shape[0] // 2
    pad_down = -(-half_down // 16) * 16
    local = planes * pad_down

    y, z, x, c = (lax.axis_index(name) for name in ("y", "z", "x", "c"))
    rank = 4 * c + 2 * x + y
    shard = 2 * x + c
    other = [0, 4, 2, 6]
    boundary = lax.dynamic_index_in_dim(bounds, z, 0, False)
    info = jnp.stack([rank, boundary])

    def to_column_owners(pieces):
        got = [
            hop_if(lax.dynamic_index_in_dim(pieces, jnp.bitwise_xor(rank, j), 0, False), j)
            for j in other
        ]
        stacked = jnp.stack(got)
        return jnp.concatenate(
            [
                lax.dynamic_index_in_dim(stacked, jnp.bitwise_xor(shard, k), 0, False)
                for k in range(4)
            ]
        )

    def hop_if(block, j):
        return hop(block, j) if j else block

    def to_row_owners(total):
        blocks = total.astype(BF16).reshape(4, own_rows, -1)
        got = [
            hop_if(lax.dynamic_index_in_dim(blocks, jnp.bitwise_xor(shard, k), 0, False), j)
            for k, j in enumerate(other)
        ]
        mine = jnp.stack([got[0], got[2], got[1], got[3]])
        theirs = hop(mine, 1)
        relative = [mine[0], theirs[0], mine[1], theirs[1], mine[2], theirs[2], mine[3], theirs[3]]
        return jnp.stack(absolute(relative, rank))

    qkv_pieces = weight_qkv.reshape(own_rows, 3, 8, 2, HD).transpose(2, 0, 3, 1, 4)
    qkv_plane = to_column_owners(qkv_pieces.reshape(8, own_rows, 6 * HD))
    out_pieces = weight_out.reshape(own_rows, 8, piece).transpose(1, 0, 2)
    out_plane = to_column_owners(out_pieces)

    def hidden_pieces(weight):
        split = weight.reshape(own_rows, planes, 2, 2, 2, half_down)
        split = split.transpose(3, 2, 4, 0, 1, 5)
        split = jnp.pad(split, [(0, 0)] * 5 + [(0, pad_down - half_down)])
        return split.reshape(8, own_rows, local)

    pair_plane = to_column_owners(
        jnp.concatenate([hidden_pieces(weight_gate), hidden_pieces(weight_up)], axis=2)
    )
    down_own = lax.dynamic_slice_in_dim(weight_down, y * half_down, half_down, 0)
    down_own = jnp.pad(down_own, [(0, pad_down - half_down), (0, 0)])

    full_qkv = ring_gather(qkv_plane, z, planes).reshape(width, 6 * HD)
    cols_out = ring_gather(out_plane, z, planes).reshape(width, piece)
    full_pair = ring_gather(pair_plane, z, planes).reshape(width, 2 * local)
    full_down = ring_gather(down_own, z, planes).reshape(local, width)
    full_out = jnp.concatenate(absolute(gather_plane(cols_out), rank), axis=1)
    gains = lax.all_gather(
        jnp.stack([norm_attn, norm_ffn]), ("z", "x", "c"), axis=1, tiled=True
    ).astype(F32)
    gain_attn, gain_ffn = gains[0], gains[1]

    inputs = tokens[0].astype(F32)
    all_tokens = jnp.concatenate(gather_plane(tokens[0])).astype(F32)
    top_all = jnp.concatenate(gather_plane(cotangent[0]))
    inv_all = lax.rsqrt(jnp.mean(all_tokens * all_tokens, axis=-1, keepdims=True) + EPS)
    inv_attn = inv_all[:rows]
    act_attn = (all_tokens * inv_all * gain_attn).astype(BF16)

    blocks = jnp.asarray([place_of(i) for i in range(8)], jnp.int32)
    blocks = jnp.take(blocks, jnp.bitwise_xor(jnp.arange(8, dtype=jnp.int32), rank))
    positions = (blocks[:, None] * rows + jnp.arange(rows, dtype=jnp.int32)[None, :]).reshape(-1)
    frequency = THETA ** (-jnp.arange(HD // 2, dtype=F32) * 2.0 / HD)
    angles = positions.astype(F32)[:, None] * frequency[None, :]
    cosine = jnp.cos(angles)
    sine = jnp.sin(angles)
    cosine = jnp.concatenate([cosine, cosine], axis=1)
    sine = jnp.concatenate([-sine, sine], axis=1)

    proj = jnp.dot(act_attn, full_qkv, preferred_element_type=F32)
    qkv, attn, lse = attend(info, proj, cosine, sine, rows)
    attn_rows = exchange_plane([attn[j * rows : (j + 1) * rows] for j in range(8)])
    attn_rows = jnp.concatenate(absolute(attn_rows, rank), axis=1)
    middle = inputs + jnp.dot(attn_rows, full_out, preferred_element_type=F32)
    inv_ffn = lax.rsqrt(jnp.mean(middle * middle, axis=-1, keepdims=True) + EPS)
    base_ffn = middle * inv_ffn
    act_own = (base_ffn * gain_ffn).astype(BF16)
    act_ffn = jnp.concatenate(gather_plane(act_own))
    pair = jnp.dot(act_ffn, full_pair, preferred_element_type=F32)
    gate_proj, up_proj = pair[:, :local], pair[:, local:]
    sigmoid_gate = jax.nn.sigmoid(gate_proj)
    silu_gate = gate_proj * sigmoid_gate
    hidden = (silu_gate * up_proj).astype(BF16)
    half = 4 * rows
    far_out = jnp.dot(hidden[half:], full_down, preferred_element_type=F32).astype(BF16)
    near_out = jnp.dot(hidden[:half], full_down, preferred_element_type=F32).astype(BF16)
    block_out = middle + scatter_plane(near_out, far_out)

    grad_down = lax.dot_general(hidden, top_all, TN, preferred_element_type=F32)
    sum_down = ring_scatter(
        grad_down.astype(BF16).reshape(planes, pad_down, width), z, planes
    )
    sum_down = sum_down[:half_down].astype(BF16)
    down_halves = absolute([sum_down, hop(sum_down, 1)], y)
    sum_down = jnp.concatenate(down_halves).astype(F32)

    grad_hidden = lax.dot_general(top_all, full_down, NT, preferred_element_type=F32)
    grad_gate = grad_hidden * up_proj * sigmoid_gate * (1.0 + gate_proj * (1.0 - sigmoid_gate))
    grad_up = grad_hidden * silu_gate
    grad_pair = jnp.concatenate([grad_gate.astype(BF16), grad_up.astype(BF16)], axis=1)
    far_act = lax.dot_general(grad_pair[half:], full_pair, NT, preferred_element_type=F32)
    near_act = lax.dot_general(grad_pair[:half], full_pair, NT, preferred_element_type=F32)
    grad_act = scatter_plane(near_act.astype(BF16), far_act.astype(BF16))
    grad_both = lax.dot_general(act_ffn, grad_pair, TN, preferred_element_type=F32)
    sum_both = ring_scatter(
        grad_both.astype(BF16).reshape(planes, 4 * own_rows, 2 * local), z, planes
    )
    sum_both = to_row_owners(sum_both)

    def whole_hidden(parts):
        split = parts.reshape(2, 2, 2, own_rows, planes, pad_down)[..., :half_down]
        split = split.transpose(3, 4, 1, 0, 2, 5)
        return split.reshape(own_rows, hidden_width).astype(F32)

    sum_gate = whole_hidden(sum_both[:, :, :local])
    sum_up = whole_hidden(sum_both[:, :, local:])

    grad_gain_ffn = jnp.sum(grad_act * base_ffn, axis=0)
    scaled_ffn = grad_act * gain_ffn
    grad_middle = (
        cotangent[0].astype(F32)
        + inv_ffn * scaled_ffn
        - middle * inv_ffn**3 * jnp.mean(scaled_ffn * middle, axis=-1, keepdims=True)
    )

    grad_branch = grad_middle.astype(BF16)

    def by_rank(value):
        columns = value.reshape(rows, 8, piece).transpose(1, 0, 2)
        return [
            lax.dynamic_index_in_dim(columns, jnp.bitwise_xor(rank, j), 0, False) for j in range(8)
        ]

    grad_attn = lax.dot_general(grad_branch, full_out, NT, preferred_element_type=F32)
    grad_heads = jnp.concatenate(exchange_plane(by_rank(grad_attn.astype(BF16))))
    grad_qkv_rows = attend_back(info, qkv, grad_heads, lse, cosine, sine, rows)

    branch_cols = jnp.concatenate(exchange_plane(by_rank(grad_branch)))
    attn_all = gather_plane(attn)
    attn_all = [
        jnp.concatenate(
            [attn_all[i][(i ^ j) * rows : ((i ^ j) + 1) * rows] for j in range(8)]
        )
        for i in range(8)
    ]
    grad_out = [
        lax.dot_general(attn_all[i], branch_cols, TN, preferred_element_type=F32).astype(BF16)
        for i in range(8)
    ]
    grad_out = jnp.concatenate(absolute(grad_out, rank))
    sum_out = ring_scatter(grad_out.reshape(planes, 4 * own_rows, piece), z, planes)
    sum_out = to_row_owners(sum_out)
    sum_out = sum_out.transpose(1, 0, 2).reshape(own_rows, width).astype(F32)

    grad_qkv = lax.dot_general(act_attn, grad_qkv_rows, TN, preferred_element_type=F32)
    sum_qkv = ring_scatter(
        grad_qkv.astype(BF16).reshape(planes, 4 * own_rows, 6 * HD), z, planes
    )
    sum_qkv = to_row_owners(sum_qkv).reshape(8, own_rows, 2, 3, HD)
    sum_qkv = sum_qkv.transpose(1, 3, 0, 2, 4).reshape(own_rows, 3 * width).astype(F32)

    far_in = lax.dot_general(grad_qkv_rows[half:], full_qkv, NT, preferred_element_type=F32)
    near_in = lax.dot_general(grad_qkv_rows[:half], full_qkv, NT, preferred_element_type=F32)
    grad_act_attn = scatter_plane(near_in.astype(BF16), far_in.astype(BF16))
    grad_gain_attn = jnp.sum(grad_act_attn * (inputs * inv_attn), axis=0)
    scaled_attn = grad_act_attn * gain_attn
    grad_tokens = (
        grad_middle
        + inv_attn * scaled_attn
        - inputs * inv_attn**3 * jnp.mean(scaled_attn * inputs, axis=-1, keepdims=True)
    )
    sum_gains = lax.psum(jnp.stack([grad_gain_attn, grad_gain_ffn]), ("y", "z", "x", "c"))
    sum_gains = lax.dynamic_slice_in_dim(sum_gains, (4 * z + shard) * own_rows, own_rows, 1)
    return (
        block_out.astype(BF16)[None],
        grad_tokens[None],
        sum_gains[0],
        sum_qkv,
        sum_out,
        sum_gains[1],
        sum_gate,
        sum_up,
        sum_down,
    )


def solution(mesh):
    shards = mesh.shape["fsdp"]
    planes = shards // 4
    grid = Mesh(mesh.devices.reshape(2, planes, 2, 2), ("y", "z", "x", "c"))
    fsdp = ("z", "x", "c")
    by_token = P(fsdp, "y", None)
    by_row = P(fsdp, None)
    return jax.shard_map(
        functools.partial(on_device, (planes, shards)),
        mesh=grid,
        in_specs=(
            by_token,
            P(),
            P(fsdp),
            by_row,
            by_row,
            P(fsdp),
            by_row,
            by_row,
            by_row,
            by_token,
        ),
        out_specs=(
            by_token,
            by_token,
            P(fsdp),
            by_row,
            by_row,
            P(fsdp),
            by_row,
            by_row,
            by_row,
        ),
        check_vma=False,
    )
```

```python
import functools

import jax
import jax.numpy as jnp
from jax import lax
from jax.experimental import pallas as pl
from jax.experimental.pallas import tpu as pltpu
from jax.sharding import Mesh, PartitionSpec as P

HD = 128
WINDOW = 1024
EPS = 1e-05
NEG = -1e30
THETA = 10000.0
F32 = jnp.float32
BF16 = jnp.bfloat16
BITS = (("y", 1), ("x", 2), ("c", 4))
SHARD_TO_RANK = (0, 4, 2, 6)
NT = (((1,), (1,)), ((), ()))
TN = (((0,), (0,)), ((), ()))
VMEM_LIMIT = 56 * 2**20
RANK, BOUND, SHARD, PLANES = 0, 1, 2, 3


def shape(dims, dtype):
    return jax.ShapeDtypeStruct(tuple(dims), dtype)


def after(value, *earlier):
    return lax.optimization_barrier((value, *earlier))[0]


def call(kernel, info, grid, in_specs, out_specs, out_shape, operands, name, flops, scratch=()):
    traffic = sum(a.size * a.dtype.itemsize for a in operands)
    traffic += sum(s.size * s.dtype.itemsize for s in jax.tree.leaves(out_shape))
    cost = int(1.2e9 + 230 * traffic)
    return pl.pallas_call(
        kernel,
        grid_spec=pltpu.PrefetchScalarGridSpec(
            num_scalar_prefetch=1,
            grid=grid,
            in_specs=in_specs,
            out_specs=out_specs,
            scratch_shapes=scratch,
        ),
        out_shape=out_shape,
        compiler_params=pltpu.CompilerParams(vmem_limit_bytes=VMEM_LIMIT),
        cost_estimate=pl.CostEstimate(flops=cost, bytes_accessed=1, transcendentals=0),
        name=name,
    )(info, *operands)


def whole(array):
    dims = array.shape
    return pl.BlockSpec(dims, lambda *_: (0,) * len(dims))


def dot(a, b):
    return jnp.dot(a, b, preferred_element_type=F32)


def dot_nt(a, b):
    return lax.dot_general(a, b, NT, preferred_element_type=F32)


def dot_tn(a, b):
    return lax.dot_general(a, b, TN, preferred_element_type=F32)


def hop(block, j):
    if not j:
        return block
    axes = tuple(name for name, bit in BITS if j & bit)
    last = 2 ** len(axes) - 1
    return lax.ppermute(block, axes, [(i, last - i) for i in range(last + 1)])


def ring_of(size):
    odd = [i for i in range(size) if i % 2 == 1]
    even = [i for i in range(size) if i % 2 == 0 and i > 0]
    return [0] + odd + even[::-1]


class Order:
    def __init__(self):
        self.gate = ()

    def do(self, function, info, *operands, **options):
        result = function(after(info, *self.gate), *operands, **options)
        self.gate = (jax.tree.leaves(result)[0],)
        return result

    def need(self, *moved):
        self.gate = self.gate + moved

    def then(self, value):
        return after(value, *self.gate) if self.gate else value


class Lane:
    def __init__(self, size):
        ring = ring_of(size)
        self.size = size
        self.route = [(ring[i], ring[(i + 1) % size]) for i in range(size)]
        self.last = ()

    def hop(self, block):
        if self.last:
            block = after(block, *self.last)
        moved = lax.ppermute(block, "z", self.route)
        self.last = (moved,)
        return moved

    def gather(self, block, steps=None):
        held = block if isinstance(block, list) else [block]
        for _ in range(steps or self.size - len(held)):
            held.append(self.hop(held[-1]))
        return held


class Sum:
    def __init__(self, order, lane, chunks):
        self.order, self.lane, self.total, self.rest = order, lane, chunks[0], list(chunks[1:])

    def move(self):
        if self.rest:
            moved = self.order.then(self.lane.hop(self.total)).astype(F32)
            self.total = (moved + self.rest.pop(0).astype(F32)).astype(BF16)
            self.order.need(self.total)

    def finish(self):
        while self.rest:
            self.move()


def near_parts(block, before_y=(), before_x=(), before_halves=()):
    half = block.shape[0] // 2
    from_y = hop(after(block, *before_y), 1)
    from_x = hop(after(block, *before_x), 2)
    first, second = after((from_y[:half], from_x[half:]), *before_halves)
    return [block, from_y, from_x, hop(first, 2), hop(second, 1)]


def join_kernel(cuts, info, *refs):
    count = len(cuts)
    out, sems = refs[count], refs[count + 1]
    copies, start = [], 0
    for i, (first, rows) in enumerate(cuts):
        source = refs[i].at[pl.ds(first, rows), :]
        copies.append(pltpu.make_async_copy(source, out.at[pl.ds(start, rows), :], sems.at[i]))
        start += rows
    for copy in copies:
        copy.start()
    for copy in copies:
        copy.wait()


def join(info, *blocks):
    blocks = [b if isinstance(b, tuple) else (b, 0, b.shape[0]) for b in blocks]
    arrays = [b[0] for b in blocks]
    cuts = tuple(b[1:] for b in blocks)
    out = shape((sum(rows for _, rows in cuts), arrays[0].shape[1]), arrays[0].dtype)
    anywhere = pl.BlockSpec(memory_space=pl.ANY)
    return call(
        functools.partial(join_kernel, cuts),
        info, (1,), [anywhere] * len(arrays), whole(out), out, arrays, "join", 0,
        [pltpu.SemaphoreType.DMA((len(arrays),))],
    )


def combine_kernel(info, near, moved, own, *outs):
    own[...] = near[0].astype(F32) + moved[0].astype(F32)
    for j, out in enumerate(outs):
        out[...] = (near[j + 1].astype(F32) + moved[j + 1].astype(F32)).astype(BF16)


def combine(info, near, moved):
    near = near.reshape(4, -1, near.shape[-1])
    moved = moved.reshape(near.shape)
    rows, columns = near.shape[1:]
    part = rows // 4
    outs = [shape((rows, columns), F32)] + [shape((rows, columns), BF16)] * 3
    source = pl.BlockSpec((4, part, columns), lambda i, s: (0, i, 0))
    return call(
        combine_kernel,
        info, (4,), [source, source], [pl.BlockSpec((part, columns), lambda i, s: (i, 0))] * 4,
        outs, (near, moved), "combine", 0,
    )


def near_moves(blocks):
    return [hop(block, j) for j, block in enumerate(blocks)]


def scatter_moves(own, *terms):
    return own, [hop(term, j + 1) for j, term in enumerate(terms)]


def meet_kernel(info, near, moved, *outs):
    rows = outs[0].shape[0] // 2
    for j, out in enumerate(outs):
        out[:rows, :] = near[j * rows : (j + 1) * rows, :]
        out[rows:, :] = moved[j * rows : (j + 1) * rows, :]


def meet(info, near, moved):
    outs = [shape((near.shape[0] // 2, near.shape[1]), near.dtype)] * 4
    return call(
        meet_kernel,
        info, (1,), [whole(near), whole(moved)], [whole(a) for a in outs], outs, (near, moved),
        "meet", 0,
    )


def pack_kernel(piece, width, info, weight_qkv, weight_out, gain, *outs):
    for k, j in enumerate(SHARD_TO_RANK):
        rank = jnp.bitwise_xor(info[RANK], j)
        for head in range(piece // HD):
            for part in range(3):
                start = pl.multiple_of(part * width + rank * piece + head * HD, HD)
                column = (head * 3 + part) * HD
                value = weight_qkv[:, pl.ds(start, HD)].astype(F32) * gain[...]
                outs[k][:, column : column + HD] = value.astype(BF16)
        outs[k][:, 3 * piece :] = weight_out[:, pl.ds(pl.multiple_of(rank * piece, piece), piece)]


def pack(info, weight_qkv, weight_out, gain):
    rows, width = weight_out.shape
    piece = width // 8
    outs = [shape((rows, 4 * piece), BF16)] * 4
    operands = (weight_qkv, weight_out, gain)
    return call(
        functools.partial(pack_kernel, piece, width),
        info, (1,), [whole(a) for a in operands], [whole(a) for a in outs], outs, operands,
        "pack", 0,
    )


def join_two_kernel(count, info, *refs):
    first, second = refs[count:]
    columns = first.shape[1]
    rows = refs[0].shape[0]
    for k in range(count):
        first[k * rows : (k + 1) * rows, :] = refs[k][:, :columns]
        second[k * rows : (k + 1) * rows, :] = refs[k][:, columns:]


def join_two(info, columns, *blocks):
    rows = sum(block.shape[0] for block in blocks)
    outs = [shape((rows, columns), BF16), shape((rows, blocks[0].shape[1] - columns), BF16)]
    return call(
        functools.partial(join_two_kernel, len(blocks)),
        info, (1,), [whole(a) for a in blocks], [whole(a) for a in outs], outs, blocks,
        "join_two", 0,
    )


def place_rows(info, parts, out):
    rows = parts[0].shape[0] // 4
    for s, source in enumerate(parts):
        for k in range(4):
            block = info[PLANES + s] * 4 + jnp.bitwise_xor(info[SHARD], k)
            out[pl.ds(pl.multiple_of(block * rows, rows), rows), :] = source[
                k * rows : (k + 1) * rows, :
            ]


def assemble_kernel(info, *refs):
    place_rows(info, refs[:-1], refs[-1])


def assemble(info, *parts):
    out = shape((len(parts) * parts[0].shape[0], parts[0].shape[1]), BF16)
    return call(
        assemble_kernel,
        info, (1,), [whole(a) for a in parts], whole(out), out, parts, "assemble", 0,
    )


def stack_kernel(count, cut, info, *refs):
    first, second = refs[count:]
    rest = refs[0].shape[0] - cut
    for s in range(count):
        plane = info[PLANES + s]
        first[pl.ds(pl.multiple_of(plane * cut, cut), cut), :] = refs[s][:cut, :]
        second[pl.ds(pl.multiple_of(plane * rest, rest), rest), :] = refs[s][cut:, :]
    for out, rows in ((first, cut), (second, rest)):
        if out.shape[0] > count * rows:
            out[count * rows :, :] = jnp.zeros((out.shape[0] - count * rows, out.shape[1]), BF16)


def stack_planes(info, cut, *parts):
    count, (rows, width) = len(parts), parts[0].shape
    outs = [
        shape((-(-count * size // 128) * 128, width), BF16) for size in (cut, rows - cut)
    ]
    return call(
        functools.partial(stack_kernel, count, cut),
        info, (1,), [whole(a) for a in parts], [whole(a) for a in outs], outs, parts, "stack", 0,
    )


def spread_kernel(count, rows, piece, info, *refs):
    out = refs[-1]
    for j in range(8):
        columns = pl.ds(
            pl.multiple_of(jnp.bitwise_xor(info[RANK], j) * piece, piece), piece
        )
        shift = 2 * ((j >> 1) & 1) + (j >> 2)
        source = refs[j // 4]
        base = (j % 4) * count * 4 * rows
        for s in range(count):
            for k in range(4):
                block = info[PLANES + s] * 4 + jnp.bitwise_xor(info[SHARD], k ^ shift)
                start = base + (s * 4 + k) * rows
                out[pl.ds(pl.multiple_of(block * rows, rows), rows), columns] = source[
                    start : start + rows, :
                ]


def spread(info, near, far, count):
    piece = near.shape[1]
    width = piece * 8
    rows = width // (4 * count)
    out = shape((width, width), BF16)
    return call(
        functools.partial(spread_kernel, count, rows, piece),
        info, (1,), [whole(near), whole(far)], whole(out), out, (near, far), "spread", 0,
    )


def project_kernel(count, info, near, far, *refs):
    parts, tables = refs[:count], refs[count : count + 4]
    weight, out, act_near, act_far = refs[count + 4 :]

    @pl.when(pl.program_id(0) == 0)
    def _():
        place_rows(info, parts, weight)

    for half, (tokens, act) in enumerate(((near, act_near), (far, act_far))):
        values = tokens[...].astype(F32)
        inverse = lax.rsqrt(jnp.mean(values * values, axis=1, keepdims=True) + EPS)
        act[...] = (values * inverse).astype(BF16)
        proj = dot(act[...], weight[...])
        for part in range(proj.shape[1] // HD):
            value = proj[:, part * HD : (part + 1) * HD]
            if part % 3 < 2:
                turned = pltpu.roll(value, HD // 2, 1)
                value = value * tables[half][...] + turned * tables[2 + half][...]
            out[half, :, part * HD : (part + 1) * HD] = value.astype(BF16)


def project(info, near, far, parts, cosine, sine):
    rows, width = near.shape
    tile = rows // 4
    columns = parts[0].shape[1]
    outs = [
        shape((width, columns), BF16),
        shape((2, rows, columns), BF16),
        shape((rows, width), BF16),
        shape((rows, width), BF16),
    ]
    tiles = pl.BlockSpec((tile, width), lambda i, s: (i, 0))
    first = pl.BlockSpec((tile, HD), lambda i, s: (i, 0))
    second = pl.BlockSpec((tile, HD), lambda i, s: (i + 4, 0))
    weight, out, act_near, act_far = call(
        functools.partial(project_kernel, len(parts)),
        info, (4,),
        [tiles, tiles]
        + [whole(a) for a in parts]
        + [first, second, first, second],
        [whole(outs[0]), pl.BlockSpec((2, tile, columns), lambda i, s: (0, i, 0)), tiles, tiles],
        outs, (near, far, *parts, cosine, cosine, sine, sine),
        "project", 4 * rows * width * columns,
    )
    return out.reshape(2 * rows, columns), weight, act_near, act_far


def place_of(block):
    return (block & 1) | ((block >> 1) & 1) << 2 | ((block >> 2) & 1) << 1


def lowest_key(block, rows, bound):
    pos = block * rows + lax.broadcasted_iota(jnp.int32, (rows, 1), 0)
    return jnp.maximum(jnp.where(pos >= bound, bound, 0), pos - (WINDOW - 1))


def block_scores(query, key, low, q_block, k_block, rows):
    scores = dot_nt(query, key) * HD**-0.5
    pos = k_block * rows + lax.broadcasted_iota(jnp.int32, (rows, rows), 1)
    seen = pos >= low
    if q_block == k_block:
        seen = seen & (
            lax.broadcasted_iota(jnp.int32, (rows, rows), 1)
            <= lax.broadcasted_iota(jnp.int32, (rows, rows), 0)
        )
    return jnp.where(seen, scores, NEG)


def key_blocks(q_block, rows):
    return range(max(0, q_block - WINDOW // rows), q_block + 1)


def row_start(block, rank, rows):
    return pl.multiple_of(jnp.bitwise_xor(place_of(block), rank) * rows, rows)


def attend_kernel(info, qkv, *refs):
    near, far, lse, result = refs
    rows = qkv.shape[0] // 8
    rank, bound = info[RANK], info[BOUND]
    for b in range(8):
        own = pl.ds(row_start(b, rank, rows), rows)
        query = qkv[own, :HD]
        low = lowest_key(b, rows, bound)
        spots = [(kb, pl.ds(row_start(kb, rank, rows), rows)) for kb in key_blocks(b, rows)]
        scores = [
            block_scores(query, qkv[at, HD : 2 * HD], low, b, kb, rows) for kb, at in spots
        ]
        top = functools.reduce(jnp.maximum, [jnp.max(s, axis=1, keepdims=True) for s in scores])
        powered = [jnp.exp(s - top) for s in scores]
        total = functools.reduce(jnp.add, [jnp.sum(p, axis=1, keepdims=True) for p in powered])
        inverse = 1.0 / total
        out = functools.reduce(
            jnp.add,
            [
                dot((p * inverse).astype(BF16), qkv[at, 2 * HD :])
                for p, (_, at) in zip(powered, spots)
            ],
        )
        result[own, :] = out.astype(BF16)
        lse[0, own, :] = top + jnp.log(total)
    near[...] = result[: 4 * rows, :]
    far[...] = result[4 * rows :, :]


def attend(info, qkv):
    length = qkv.shape[0]
    rows = length // 8
    heads = qkv.shape[1] // (3 * HD)
    outs = [shape((4 * rows, heads * HD), BF16)] * 2 + [shape((heads, length, 1), F32)]
    return call(
        attend_kernel,
        info, (heads,), [pl.BlockSpec((length, 3 * HD), lambda h, s: (0, h))],
        [pl.BlockSpec((4 * rows, HD), lambda h, s: (0, h))] * 2
        + [pl.BlockSpec((1, length, 1), lambda h, s: (h, 0, 0))],
        outs, (qkv,), "attend", 8 * heads * length * WINDOW * HD,
        [pltpu.VMEM((length, HD), BF16)],
    )


def attend_back_kernel(info, qkv, *refs):
    grads, (lse, cosine, sine, out, top_all, sum_key, sum_value) = refs[:4], refs[4:]
    rows = qkv.shape[0] // 8
    rank, bound = info[RANK], info[BOUND]
    sum_key[...] = jnp.zeros_like(sum_key)
    sum_value[...] = jnp.zeros_like(sum_value)
    for j in range(4):
        top_all[j * rows : (j + 1) * rows, :] = grads[j][:rows, :]
        top_all[(j + 4) * rows : (j + 5) * rows, :] = grads[j][rows:, :]

    def unturn(value, at):
        value = value.astype(BF16).astype(F32)
        turned = value * cosine[at, :] - pltpu.roll(value, HD // 2, 1) * sine[at, :]
        return turned.astype(BF16)

    for b in range(8):
        own = pl.ds(row_start(b, rank, rows), rows)
        query = qkv[own, :HD]
        top = top_all[own, :]
        low = lowest_key(b, rows, bound)
        log_total = lse[0, own, :]
        spots = [(kb, pl.ds(row_start(kb, rank, rows), rows)) for kb in key_blocks(b, rows)]
        probs = [
            jnp.exp(block_scores(query, qkv[at, HD : 2 * HD], low, b, kb, rows) - log_total)
            for kb, at in spots
        ]
        slopes = [dot_nt(top, qkv[at, 2 * HD :]) for _, at in spots]
        mean = functools.reduce(
            jnp.add, [jnp.sum(p * g, axis=1, keepdims=True) for p, g in zip(probs, slopes)]
        )
        sum_query = jnp.zeros((rows, HD), F32)
        for p, g, (_, at) in zip(probs, slopes, spots):
            low_grad = (p * (g - mean)).astype(BF16)
            sum_query = sum_query + dot(low_grad, qkv[at, HD : 2 * HD])
            sum_key[at, :] += dot_tn(low_grad, query)
            sum_value[at, :] += dot_tn(p.astype(BF16), top)
        out[own, :HD] = unturn(sum_query * HD**-0.5, own)

    @pl.loop(0, 8)
    def _(j):
        at = pl.ds(pl.multiple_of(j * rows, rows), rows)
        out[at, HD : 2 * HD] = unturn(sum_key[at, :] * HD**-0.5, at)
        out[at, 2 * HD :] = sum_value[at, :].astype(BF16)


def attend_back(info, qkv, grads, lse, cosine, sine, head):
    length = qkv.shape[0]
    rows = length // 8
    out = shape((length, 3 * HD), BF16)
    return call(
        attend_back_kernel,
        info, (1,),
        [pl.BlockSpec((length, 3 * HD), lambda i, s: (0, head))]
        + [pl.BlockSpec((2 * rows, HD), lambda i, s: (0, head))] * 4
        + [pl.BlockSpec((1, length, 1), lambda i, s: (head, 0, 0))]
        + [whole(cosine), whole(sine)],
        whole(out), out, (qkv, *grads, lse, cosine, sine), "attend_back",
        20 * length * WINDOW * HD,
        [
            pltpu.VMEM((length, HD), BF16),
            pltpu.VMEM((length, HD), F32),
            pltpu.VMEM((length, HD), F32),
        ],
    )


def branch_kernel(piece, info, *refs):
    blocks = refs[:4]
    weight, tokens, attn, middle, scale, act = refs[4:]
    step = pl.program_id(0)
    width = weight.shape[1]

    @pl.when(step == 0)
    def _():
        rows = tokens.shape[0]
        for j in range(8):
            start = pl.multiple_of(jnp.bitwise_xor(info[RANK], j) * piece, piece)
            first = j // 4 * rows
            attn[:, pl.ds(start, piece)] = blocks[j % 4][first : first + rows, :]

    at = pl.ds(pl.multiple_of(step * width, width), width)
    middle[:, at] = tokens[:, at].astype(F32) + dot(attn[...], weight[...])

    @pl.when(step == pl.num_programs(0) - 1)
    def _():
        value = middle[...]
        inverse = lax.rsqrt(jnp.mean(value * value, axis=1, keepdims=True) + EPS)
        scale[...] = inverse
        act[...] = (value * inverse).astype(BF16)


def branch(info, blocks, weight, tokens):
    rows, width = tokens.shape
    outs = [
        shape((rows, width), BF16),
        shape((rows, width), F32),
        shape((rows, 1), F32),
        shape((rows, width), BF16),
    ]
    return call(
        functools.partial(branch_kernel, width // 8),
        info, (4,),
        [whole(a) for a in blocks]
        + [pl.BlockSpec((width, width // 4), lambda i, s: (0, i)), whole(tokens)],
        [whole(a) for a in outs], outs, (*blocks, weight, tokens), "branch",
        2 * rows * width * width,
    )


def slopes_kernel(info, near, far, first, second, out_near, out_far):
    columns = first.shape[0]
    for top, out in ((near, out_near), (far, out_far)):
        out[:, :columns] = dot_nt(top[...], first[...])
        out[:, columns:] = dot_nt(top[...], second[...])


def slopes(info, near, far, first, second):
    rows, width = near.shape
    tile = rows // 4
    columns = first.shape[0] + second.shape[0]
    tiles = pl.BlockSpec((tile, width), lambda i, s: (i, 0))
    return call(
        slopes_kernel,
        info, (4,), [tiles, tiles, whole(first), whole(second)],
        [pl.BlockSpec((tile, columns), lambda i, s: (i, 0))] * 2,
        [shape((rows, columns), F32)] * 2, (near, far, first, second), "slopes",
        4 * rows * width * columns,
    )


def ffn_kernel(tail, more, info, *refs):
    if more:
        act, slope, pair, earlier, earlier_pair, hidden, grads, back = refs
    else:
        act, slope, pair, hidden, grads = refs
    double = pair.shape[1]
    main = double // 2 - tail
    proj = dot(act[...], pair[...])

    def gated(gate, up, grad):
        sigmoid = jax.nn.sigmoid(gate)
        silu = gate * sigmoid
        return (
            silu * up,
            grad * up * sigmoid * (1.0 + gate * (1.0 - sigmoid)),
            grad * silu,
        )

    value, to_gate, to_up = gated(proj[:, :main], proj[:, double - main :], slope[:, :main])
    hidden[:, :main] = value.astype(BF16)
    grads[:, :main] = to_gate.astype(BF16)
    grads[:, double - main :] = to_up.astype(BF16)
    if tail:
        mixed = proj[:, main : main + 2 * tail]
        value, to_gate, to_up = gated(
            mixed, pltpu.roll(mixed, tail, 1), slope[:, main : main + 2 * tail]
        )
        first = lax.broadcasted_iota(jnp.int32, mixed.shape, 1) < tail
        hidden[:, main : main + 2 * tail] = jnp.where(first, value, 0.0).astype(BF16)
        grads[:, main : main + 2 * tail] = jnp.where(
            first, to_gate, pltpu.roll(to_up, tail, 1)
        ).astype(BF16)
    if more:
        total = dot_nt(grads[...], pair[...]) + dot_nt(earlier[...], earlier_pair[...])
        back[...] = total.astype(BF16)


def ffn(info, act, slope, chunk, pair, earlier=None, earlier_pair=None):
    rows, width = act.shape
    tile = rows // 4
    double = pair.shape[1]
    columns = -(-double // 256) * 128
    offset = slope.shape[1] // columns - 1 if chunk else 0
    more = earlier is not None
    tiles = pl.BlockSpec((tile, width), lambda i, s: (i, 0))
    operands = [act, slope, pair]
    in_specs = [tiles, pl.BlockSpec((tile, columns), lambda i, s: (i, offset)), whole(pair)]
    outs = [shape((rows, columns), BF16), shape((rows, double), BF16)]
    out_specs = [
        pl.BlockSpec((tile, columns), lambda i, s: (i, 0)),
        pl.BlockSpec((tile, double), lambda i, s: (i, 0)),
    ]
    flops = 2 * rows * width * double
    if more:
        operands += [earlier, earlier_pair]
        in_specs += [
            pl.BlockSpec((tile, earlier.shape[1]), lambda i, s: (i, 0)),
            whole(earlier_pair),
        ]
        outs += [shape((rows, width), BF16)]
        out_specs += [tiles]
        flops += 2 * rows * width * (double + earlier.shape[1])
    return call(
        functools.partial(ffn_kernel, double // 2 % 128, more),
        info, (4,), in_specs, out_specs, outs, operands, "ffn", flops,
    )


def grad_rows_kernel(own_rows, info, act_near, act_far, near, far, *refs):
    outs, total = refs[:-1], refs[-1]
    total[...] = dot_tn(act_near[...], near[...]) + dot_tn(act_far[...], far[...])
    for i, out in enumerate(outs):

        @pl.when(pl.program_id(0) == i)
        def _():
            for k in range(4):
                start = jnp.bitwise_xor(info[SHARD], k) * own_rows
                value = total[pl.ds(pl.multiple_of(start, own_rows), own_rows), :]
                out[k * own_rows : (k + 1) * own_rows, :] = value.astype(BF16)


def grad_rows(info, act_near, act_far, near, far, count, name, split=False):
    rows, width = act_near.shape
    chunk = width // count
    columns = near.shape[1]

    def spot(i, s):
        return (0, s[PLANES + (i + 1) % count])

    acts = pl.BlockSpec((rows, chunk), spot)
    outs = [shape((chunk, columns), BF16)] * count
    first = pl.BlockSpec((rows, columns), lambda i, s: (0, 0))
    second = pl.BlockSpec((rows, columns), lambda i, s: (1 if split else 0, 0))
    return call(
        functools.partial(grad_rows_kernel, chunk // 4),
        info, (count,), [acts, acts, first, second], [whole(a) for a in outs], outs,
        (act_near, act_far, near, far), name, 4 * rows * width * columns,
        [pltpu.VMEM((chunk, columns), F32)],
    )


def grad_down_kernel(rows, info, first_near, first_far, second_near, second_far, *refs):
    top_near, top_far = refs[:2]
    outs, total = refs[2:-1], refs[-1]
    count = len(outs)
    start = 0
    for near, far, part in ((first_near, first_far, rows[0]), (second_near, second_far, rows[1])):
        units = near.shape[1]
        total[:units, :] = dot_tn(near[...], top_near[...]) + dot_tn(far[...], top_far[...])
        for i in range(count):
            at = pl.multiple_of(info[PLANES + (i + 1) % count] * part, part)
            outs[i][start : start + part, :] = total[pl.ds(at, part), :].astype(BF16)
        start += part


def grad_down(info, first, second, top_near, top_far, count, rows):
    tokens, width = top_near.shape
    part = width // 4
    outs = [shape((sum(rows), width), BF16)] * count
    tops = pl.BlockSpec((tokens, part), lambda i, s: (0, i))
    hidden = (*first, *second)
    units = max(a.shape[1] for a in hidden)
    return call(
        functools.partial(grad_down_kernel, rows),
        info, (4,), [whole(a) for a in hidden] + [tops, tops],
        [pl.BlockSpec((sum(rows), part), lambda i, s: (0, i))] * count, outs,
        (*hidden, top_near, top_far), "grad_down",
        4 * tokens * width * (first[0].shape[1] + second[0].shape[1]),
        [pltpu.VMEM((units, part), F32)],
    )


def matmul_two_kernel(info, a, b, c, d, out):
    out[...] = (dot(a[...], b[...]) + dot(c[...], d[...])).astype(BF16)


def down_product(info, first, second, down_first, down_second):
    rows, width = first.shape[0], down_first.shape[1]
    tile = rows // 4
    out = shape((rows, width), BF16)
    return call(
        matmul_two_kernel,
        info, (4,),
        [
            pl.BlockSpec((tile, first.shape[1]), lambda i, s: (i, 0)), whole(down_first),
            pl.BlockSpec((tile, second.shape[1]), lambda i, s: (i, 0)), whole(down_second),
        ],
        pl.BlockSpec((tile, width), lambda i, s: (i, 0)), out,
        (first, down_first, second, down_second), "down_product",
        2 * rows * width * (first.shape[1] + second.shape[1]),
    )


def grad_attn_kernel(info, *refs):
    own, first, second, third, top, middle, scale, weight = refs[:8]
    grad_middle, branch_ref, near, far = refs[8:]
    step = pl.program_id(0)
    rows = own.shape[0]

    @pl.when(step == 0)
    def _():
        grad = own[...]
        for moved in (first, second, third):
            grad = grad + moved[...].astype(F32)
        value, inverse = middle[...], scale[...]
        mean = jnp.mean(grad * value, axis=1, keepdims=True)
        total = top[...].astype(F32) + inverse * grad - value * (inverse**3 * mean)
        grad_middle[...] = total
        branch_ref[...] = total.astype(BF16)

    value = dot_nt(branch_ref[...], weight[...]).astype(BF16)
    for j in range(8):

        @pl.when(step == j)
        def _():
            out = far if j > 3 else near
            out[j % 4 * rows : (j % 4 + 1) * rows, :] = value


def grad_attn(info, own, parts, top, middle, scale, weight):
    rows, width = middle.shape
    piece = width // 8
    outs = [shape((rows, width), F32), shape((rows, width), BF16)]
    outs += [shape((4 * rows, piece), BF16)] * 2
    operands = (own, *parts, top, middle, scale)

    def spot(i, s):
        return (jnp.bitwise_xor(s[RANK], i), 0)

    return call(
        grad_attn_kernel,
        info, (8,), [whole(a) for a in operands] + [pl.BlockSpec((piece, width), spot)],
        [whole(a) for a in outs], outs, (*operands, weight), "grad_attn",
        2 * rows * width * width,
    )


def grad_out_kernel(info, attn, near_cols, far_cols, near, far):
    near[0] = dot_tn(attn[...], near_cols[...]).astype(BF16)
    far[0] = dot_tn(attn[...], far_cols[...]).astype(BF16)


def grad_out_terms(info, attn, grad):
    rows, width = attn.shape
    piece = width // 8
    outs = [shape((4, width, piece), BF16)] * 2
    return call(
        grad_out_kernel,
        info, (4,),
        [
            whole(attn),
            pl.BlockSpec((rows, piece), lambda i, s: (0, jnp.bitwise_xor(s[RANK], i))),
            pl.BlockSpec((rows, piece), lambda i, s: (0, jnp.bitwise_xor(s[RANK], i + 4))),
        ],
        [pl.BlockSpec((1, width, piece), lambda i, s: (i, 0, 0))] * 2, outs,
        (attn, grad, grad), "grad_out", 2 * rows * width * width,
    )


def order_kernel(own_rows, info, own, first, second, third, *refs):
    outs, total = refs[:-1], refs[-1]
    count = len(outs)
    value = own[...]
    for moved in (first, second, third):
        value = value + moved[...].astype(F32)
    total[...] = value
    for i, out in enumerate(outs):
        for k in range(4):
            block = info[PLANES + (i + 1) % count] * 4 + jnp.bitwise_xor(info[SHARD], k)
            value = total[pl.ds(pl.multiple_of(block * own_rows, own_rows), own_rows), :]
            out[k * own_rows : (k + 1) * own_rows, :] = value.astype(BF16)


def order_out(info, own, parts, count):
    width, columns = own.shape
    outs = [shape((width // count, columns), BF16)] * count
    return call(
        functools.partial(order_kernel, width // count // 4),
        info, (1,), [whole(a) for a in (own, *parts)], [whole(a) for a in outs], outs,
        (own, *parts), "order_out", 0, [pltpu.VMEM((width, columns), F32)],
    )


def back_product_kernel(info, first, second, weight, out):
    columns = first.shape[1]
    total = dot_nt(first[...], weight[:, :columns]) + dot_nt(second[...], weight[:, columns:])
    out[...] = total.astype(BF16)


def back_product(info, first, second, weight, far):
    rows, width = first.shape[0] // 2, weight.shape[0]
    tile = rows // 4
    out = shape((rows, width), BF16)
    tiles = pl.BlockSpec((tile, first.shape[1]), lambda i, s: (i + (4 if far else 0), 0))
    return call(
        back_product_kernel,
        info, (4,), [tiles, tiles, whole(weight)],
        pl.BlockSpec((tile, width), lambda i, s: (i, 0)), out, (first, second, weight),
        "back_product", 2 * rows * width * weight.shape[1],
    )


def rank_block(info, j, mine, theirs):
    rows = mine.shape[0] // 4
    source = theirs if j % 2 else mine
    return source[j // 2 * rows : (j // 2 + 1) * rows, :]


def finish_qkv_kernel(info, *refs):
    pairs = (refs[:2], refs[2:4])
    weight, gain, out, gain_out = refs[4:]
    rows, width = out.shape[0], out.shape[1] // 3
    total = jnp.zeros((rows, HD), F32)
    for j in range(8):
        rank = jnp.bitwise_xor(info[RANK], j)
        for head, pair in enumerate(pairs):
            block = rank_block(info, j, *pair)
            for part in range(3):
                start = pl.multiple_of(part * width + (2 * rank + head) * HD, HD)
                value = block[:, part * HD : (part + 1) * HD].astype(F32)
                out[:, pl.ds(start, HD)] = value * gain[...]
                total = total + value * weight[:, pl.ds(start, HD)].astype(F32)
    gain_out[...] = jnp.sum(total, axis=1, keepdims=True)


def finish_qkv(info, first, second, weight, gain):
    outs = [shape(weight.shape, F32), shape(gain.shape, F32)]
    operands = (*first, *second, weight, gain)
    return call(
        finish_qkv_kernel,
        info, (1,), [whole(a) for a in operands], [whole(a) for a in outs], outs, operands,
        "finish_qkv", 0,
    )


def finish_out_kernel(info, mine, theirs, out):
    piece = mine.shape[1]
    for j in range(8):
        start = pl.multiple_of(jnp.bitwise_xor(info[RANK], j) * piece, piece)
        out[:, pl.ds(start, piece)] = rank_block(info, j, mine, theirs).astype(F32)


def finish_out(info, mine, theirs):
    rows, piece = mine.shape[0] // 4, mine.shape[1]
    out = shape((rows, 8 * piece), F32)
    return call(
        finish_out_kernel,
        info, (1,), [whole(mine), whole(theirs)], whole(out), out, (mine, theirs),
        "finish_out", 0,
    )


def unit_lanes(first, count, local):
    main = local // 128 * 128
    runs = []
    while count:
        size = min(count, main - first) if first < main else count
        up = local + (local - main) + first if first < main else local + first - main
        runs.append((first, up, size))
        first, count = first + size, count - size
    return runs


def finish_pair_kernel(planes, reals, pads, info, *refs):
    chunks = (refs[:2], refs[2:4])
    weights, gain, outs, gain_out = refs[4:6], refs[6], refs[7:9], refs[9]
    held = refs[10:]
    rows, width = outs[0].shape
    half_down = sum(reals)
    for (mine, theirs), by_rank in zip(chunks, held):
        for j in range(8):
            start = jnp.bitwise_xor(info[RANK], j) * rows
            block = rank_block(info, j, mine, theirs)
            by_rank[pl.ds(pl.multiple_of(start, rows), rows), :] = block[...].astype(F32)

    def move(chunk, rank, lane, out, column, size):
        source, target = lane // 128 * 128, column // 128 * 128
        wide = 128 if (lane - source) + size <= 128 and (column - target) + size <= 128 else 256
        at = slice(rank * rows, (rank + 1) * rows)
        if (lane - source) + size <= 128:
            value = held[chunk][at, source : source + 128]
            if wide == 256:
                value = jnp.concatenate([value, value], axis=1)
        else:
            value = held[chunk][at, source : source + 256]
        shift = ((column - target) - (lane - source)) % wide
        if shift:
            value = pltpu.roll(value, shift, 1)
        lanes = lax.broadcasted_iota(jnp.int32, value.shape, 1)
        keep = (lanes >= column - target) & (lanes < column - target + size)
        spot = slice(target, min(target + wide, width))
        if target + wide > width:
            value, keep = value[:, : width - target], keep[:, : width - target]
        out[:, spot] = jnp.where(keep, value, out[:, spot])

    for plane in range(planes):
        for rank in range(8):
            shard = 2 * (rank >> 1 & 1) + (rank >> 2)
            column = ((plane * 4 + shard) * 2 + (rank & 1)) * half_down
            for chunk, (real, pad) in enumerate(zip(reals, pads)):
                start = column
                for gate, up, size in unit_lanes(plane * pad, real, planes * pad):
                    move(chunk, rank, gate, outs[0], start, size)
                    move(chunk, rank, up, outs[1], start, size)
                    start += size
                column += real
    total = jnp.zeros((rows, 128), F32)
    for weight, out in zip(weights, outs):
        for tile in range(width // 128):
            at = slice(tile * 128, (tile + 1) * 128)
            value = out[:, at]
            total = total + value * weight[:, at].astype(F32)
            out[:, at] = value * gain[...]
    gain_out[...] = jnp.sum(total, axis=1, keepdims=True)


def finish_pair(info, first, second, gate, up, gain, planes, reals, pads):
    rows = gate.shape[0]
    outs = [shape(gate.shape, F32)] * 2 + [shape(gain.shape, F32)]
    operands = (*first, *second, gate, up, gain)
    return call(
        functools.partial(finish_pair_kernel, planes, reals, pads),
        info, (1,), [whole(a) for a in operands], [whole(a) for a in outs], outs, operands,
        "finish_pair", 0,
        [pltpu.VMEM((8 * rows, pair[0].shape[1]), F32) for pair in (first, second)],
    )


def on_device(
    planes,
    tokens,
    bounds,
    norm_attn,
    weight_qkv,
    weight_out,
    norm_ffn,
    weight_gate,
    weight_up,
    weight_down,
    cotangent,
):
    rows, width = tokens.shape[1], tokens.shape[2]
    own_rows = weight_qkv.shape[0]
    half_down = weight_down.shape[0] // 2
    cut = -(-half_down // 32) * 16
    pads = (cut, -(-(half_down - cut) // 16) * 16)
    reals = (cut, half_down - cut)
    starts = (0, cut)

    y, z, x, c = (lax.axis_index(name) for name in ("y", "z", "x", "c"))
    rank = 4 * c + 2 * x + y
    shard = 2 * x + c
    ring_list = ring_of(planes)
    table = [
        [ring_list[(ring_list.index(i) - s) % planes] for s in range(planes)]
        for i in range(planes)
    ]
    arrival = jnp.asarray(table, jnp.int32)[z]
    boundary = lax.dynamic_index_in_dim(bounds, z, 0, False)
    info = jnp.concatenate([jnp.stack([rank, boundary, shard]).astype(jnp.int32), arrival])
    order = Order()
    do, need = order.do, order.need
    lane_a, lane_b = Lane(planes), Lane(planes)

    def spread_pieces(pieces):
        return [hop(piece, j) for piece, j in zip(pieces, SHARD_TO_RANK)]

    def owners(total):
        return [
            hop(total[k * own_rows : (k + 1) * own_rows], SHARD_TO_RANK[k]) for k in (2, 1, 3)
        ]

    def rows_of(total, pieces):
        need(*pieces)
        mine = do(join, info, (total, 0, own_rows), *pieces)
        return mine, hop(mine, 1)

    down_own = lax.dynamic_slice_in_dim(weight_down, y * half_down, half_down, 0)
    down_own = jnp.pad(down_own, [(0, sum(pads) - half_down), (0, 0)])
    down_got = lane_a.gather(down_own, 1)
    wide_attn = norm_attn.astype(F32)[:, None]
    wide_ffn = norm_ffn.astype(F32)[:, None]
    pieces = spread_pieces(do(pack, info, weight_qkv, weight_out, wide_attn))
    token_parts = near_parts(tokens[0], (), pieces[1:])

    def split_hidden(weight):
        split = (after(weight, *pieces).astype(F32) * wide_ffn).astype(BF16)
        split = split.reshape(own_rows, planes, 2, 2, 2, half_down)
        return split.transpose(3, 2, 4, 0, 1, 5).reshape(8, own_rows, planes, half_down)

    gate_split, up_split = split_hidden(weight_gate), split_hidden(weight_up)
    pair_pieces = []
    for start, real, pad in zip(starts, reals, pads):
        both = []
        for split in (gate_split, up_split):
            part = split[..., start : start + real]
            part = jnp.pad(part, [(0, 0)] * 3 + [(0, pad - real)])
            both.append(part.reshape(8, own_rows, planes * pad))
        main = planes * pad // 128 * 128
        pair_pieces += [both[0], both[1][..., main:], both[1][..., :main]]
    pair_pieces = jnp.concatenate(pair_pieces, axis=-1)
    pair_pieces = spread_pieces(
        [
            lax.dynamic_index_in_dim(pair_pieces, jnp.bitwise_xor(rank, j), 0, False)
            for j in SHARD_TO_RANK
        ]
    )

    blocks = jnp.asarray([place_of(i) for i in range(8)], jnp.int32)
    blocks = jnp.take(blocks, jnp.bitwise_xor(jnp.arange(8, dtype=jnp.int32), rank))
    positions = (blocks[:, None] * rows + jnp.arange(rows, dtype=jnp.int32)[None, :]).reshape(-1)
    frequency = THETA ** (-jnp.arange(HD // 2, dtype=F32) * 2.0 / HD)
    angles = positions.astype(F32)[:, None] * frequency[None, :]
    cosine = jnp.cos(angles)
    sine = jnp.sin(angles)
    cosine = jnp.concatenate([cosine, cosine], axis=1)
    sine = jnp.concatenate([-sine, sine], axis=1)

    need(down_got[1], *pieces[1:])
    qkv_plane, out_plane = do(join_two, info, 3 * (width // 8), *pieces)
    out_got = lane_a.gather(out_plane)
    qkv_got = lane_b.gather(qkv_plane)
    need(out_got[1], *pair_pieces[1:])
    pair_first, pair_second = do(join_two, info, 2 * planes * pads[0], *pair_pieces)
    need(*out_got, qkv_got[1])
    out_cols = do(join, info, *out_got)
    out_parts = near_parts(out_cols, token_parts[1:2], pair_pieces, token_parts)
    need(*token_parts)
    tokens_near = do(join, info, *token_parts)
    tokens_far = hop(tokens_near, 4)
    lane_a.last = (qkv_got[-1],)
    pair_first_got = lane_b.gather(pair_first)
    down_got = lane_a.gather(down_got)
    pair_second_got = lane_a.gather(pair_second)
    need(tokens_far, *qkv_got)
    qkv, full_qkv, act_near, act_far = do(
        project, info, tokens_near, tokens_far, qkv_got, cosine, sine
    )
    need(*out_parts)
    out_near = do(join, info, *out_parts)
    out_far = hop(out_near, 4)
    top_parts = near_parts(after(cotangent[0], *out_parts))
    attn_near, attn_far, lse = do(attend, info, qkv)
    moved = hop(attn_far, 4)
    need(out_far, down_got[2], pair_first_got[1])
    full_out = do(spread, info, out_near, out_far, planes)
    need(moved)
    attn_moved = near_moves(do(meet, info, attn_near, moved))
    need(*attn_moved)
    attn, middle, scale, act_own = do(branch, info, attn_moved, full_out, tokens[0])
    act_parts = near_parts(act_own)
    need(*top_parts, pair_first_got[2])
    top_near = do(join, info, *top_parts)
    top_far = hop(top_near, 4)
    need(*down_got)
    down_a, down_b = do(stack_planes, info, pads[0], *down_got)
    need(top_far)
    slope_near, slope_far = do(slopes, info, top_near, top_far, down_a, down_b)
    need(*pair_first_got, pair_second_got[1])
    full_first = do(assemble, info, *pair_first_got)
    need(*act_parts)
    ffn_near = do(join, info, *act_parts)
    ffn_far = hop(ffn_near, 4)

    hidden_near, grads_near = do(ffn, info, ffn_near, slope_near, 0, full_first)
    need(ffn_far, pair_second_got[2])
    hidden_far, grads_far = do(ffn, info, ffn_far, slope_far, 0, full_first)
    lane_c = Lane(planes)
    pair_a = Sum(
        order,
        lane_b,
        do(grad_rows, info, ffn_near, ffn_far, grads_near, grads_far, planes, "grad_pair"),
    )
    need(*pair_second_got)
    full_second = do(assemble, info, *pair_second_got)
    second_far, more_far, far_terms = do(
        ffn, info, ffn_far, slope_far, 1, full_second, grads_far, full_first
    )
    moved = hop(far_terms, 4)
    second_near, more_near, near_terms = do(
        ffn, info, ffn_near, slope_near, 1, full_second, grads_near, full_first
    )
    pair_a.move()
    need(moved)
    own, parts = scatter_moves(*do(combine, info, near_terms, moved))
    pair_b = Sum(
        order,
        lane_a,
        do(grad_rows, info, ffn_near, ffn_far, more_near, more_far, planes, "grad_pair"),
    )
    pair_a.move()
    down_sum = Sum(
        order,
        lane_b,
        do(
            grad_down, info, (hidden_near, hidden_far), (second_near, second_far),
            top_near, top_far, planes, pads,
        ),
    )
    block_near = do(down_product, info, hidden_near, second_near, down_a, down_b)
    need(*parts)

    grad_middle, grad_branch, attn_near, attn_far = do(
        grad_attn, info, own, parts, cotangent[0], middle, scale, full_out
    )
    pair_a.move()
    away = hop(attn_far, 4)
    near_out, far_out = do(grad_out_terms, info, attn, grad_branch)
    pair_b.move()
    first_pieces = owners(pair_a.total)
    need(away)
    attn_grads = near_moves(do(meet, info, attn_near, away))
    out_moved = hop(after(far_out, attn_grads[0]), 4)
    need(*first_pieces)
    block_far = do(down_product, info, hidden_far, second_far, down_a, down_b)
    need(*attn_grads)
    grads_first = do(attend_back, info, qkv, attn_grads, lse, cosine, sine, 0)
    pair_b.move()
    sums_first = rows_of(pair_a.total, first_pieces)
    need(out_moved)
    out_own, out_parts = scatter_moves(*do(combine, info, near_out, out_moved))
    down_sum.move()
    qkv_first = Sum(
        order,
        lane_a,
        do(grad_rows, info, act_near, act_far, grads_first, grads_first, planes, "grad_qkv", True),
    )
    block_moved = hop(after(block_far, qkv_first.total), 4)
    pair_b.move()
    grads_second = do(attend_back, info, qkv, attn_grads, lse, cosine, sine, 1)
    second_pieces = owners(pair_b.total)
    down_sum.move()
    need(block_moved)
    block_terms = do(combine, info, block_near, block_moved)
    qkv_first.move()
    need(*second_pieces)
    sums_second = rows_of(pair_b.total, second_pieces)
    qkv_second = Sum(
        order,
        lane_b,
        do(
            grad_rows, info, act_near, act_far, grads_second, grads_second, planes,
            "grad_qkv", True,
        ),
    )
    block_own, block_parts = scatter_moves(block_terms[0], *after(block_terms[1:], *out_parts))
    down_sum.move()

    in_far = do(back_product, info, grads_first, grads_second, full_qkv, True)
    in_moved = hop(in_far, 4)
    qkv_first.move()
    down_mine = down_sum.total[:half_down]
    down_theirs = hop(down_mine, 1)
    in_near = do(back_product, info, grads_first, grads_second, full_qkv, False)
    need(*out_parts)
    out_sum = Sum(order, lane_c, do(order_out, info, out_own, out_parts, planes))
    qkv_second.move()
    need(in_moved, *block_parts)
    in_own, in_parts = scatter_moves(*do(combine, info, in_near, in_moved))
    qkv_first.move()
    out_sum.move()
    need(*sums_first, *sums_second)
    sum_gate, sum_up, gain_sum_ffn = do(
        finish_pair, info, sums_first, sums_second, weight_gate, weight_up, wide_ffn,
        planes, reals, pads,
    )
    first_pieces = owners(qkv_first.total)
    qkv_second.move()
    out_sum.finish()
    first_rows = rows_of(qkv_first.total, first_pieces)
    out_pieces = owners(out_sum.total)
    qkv_second.finish()
    second_pieces = owners(qkv_second.total)
    out_rows = rows_of(out_sum.total, out_pieces)
    second_rows = rows_of(qkv_second.total, second_pieces)

    down_both = jnp.stack([down_mine, down_theirs])
    sum_down = jnp.concatenate(
        [lax.dynamic_index_in_dim(down_both, jnp.bitwise_xor(y, i), 0, False) for i in range(2)]
    ).astype(F32)
    need(out_rows[1])
    sum_out = do(finish_out, info, *out_rows)
    need(first_rows[1], second_rows[1])
    sum_qkv, gain_sum_attn = do(
        finish_qkv, info, first_rows, second_rows, weight_qkv, wide_attn
    )
    block_out = middle + block_own + sum(part.astype(F32) for part in block_parts)
    inputs = tokens[0].astype(F32)
    inv_attn = lax.rsqrt(jnp.mean(inputs * inputs, axis=-1, keepdims=True) + EPS)
    scaled = in_own + sum(part.astype(F32) for part in in_parts)
    grad_tokens = (
        grad_middle
        + inv_attn * scaled
        - inputs * inv_attn**3 * jnp.mean(scaled * inputs, axis=-1, keepdims=True)
    )
    return (
        block_out.astype(BF16)[None],
        grad_tokens[None],
        gain_sum_attn[:, 0],
        sum_qkv,
        sum_out,
        gain_sum_ffn[:, 0],
        sum_gate,
        sum_up,
        sum_down,
    )


def solution(mesh):
    planes = mesh.shape["fsdp"] // 4
    grid = Mesh(mesh.devices.reshape(2, planes, 2, 2), ("y", "z", "x", "c"))
    fsdp = ("z", "x", "c")
    by_token = P(fsdp, "y", None)
    by_row = P(fsdp, None)
    gain = P(fsdp)
    return jax.shard_map(
        functools.partial(on_device, planes),
        mesh=grid,
        in_specs=(
            by_token, P(), gain, by_row, by_row, gain, by_row, by_row, by_row, by_token,
        ),
        out_specs=(
            by_token, by_token, gain, by_row, by_row, gain, by_row, by_row, by_row,
        ),
        check_vma=False,
    )
```

```python
import functools

import jax
import jax.numpy as jnp
from jax import lax
from jax.experimental import pallas as pl
from jax.experimental.pallas import tpu as pltpu
from jax.sharding import Mesh, PartitionSpec as P

HD = 128
WINDOW = 1024
EPS = 1e-05
NEG = -1e30
THETA = 10000.0
F32 = jnp.float32
BF16 = jnp.bfloat16
BITS = (("y", 1), ("x", 2), ("c", 4))
SHARD_TO_RANK = (0, 4, 2, 6)
NT = (((1,), (1,)), ((), ()))
TN = (((0,), (0,)), ((), ()))
VMEM_LIMIT = 56 * 2**20
RANK, BOUND, SHARD, PLANES = 0, 1, 2, 3


def shape(dims, dtype):
    return jax.ShapeDtypeStruct(tuple(dims), dtype)


def after(value, *earlier):
    return lax.optimization_barrier((value, *earlier))[0]


def call(kernel, info, grid, in_specs, out_specs, out_shape, operands, name, flops, scratch=()):
    traffic = sum(a.size * a.dtype.itemsize for a in operands)
    traffic += sum(s.size * s.dtype.itemsize for s in jax.tree.leaves(out_shape))
    cost = int(1.2e9 + 230 * traffic)
    return pl.pallas_call(
        kernel,
        grid_spec=pltpu.PrefetchScalarGridSpec(
            num_scalar_prefetch=1,
            grid=grid,
            in_specs=in_specs,
            out_specs=out_specs,
            scratch_shapes=scratch,
        ),
        out_shape=out_shape,
        compiler_params=pltpu.CompilerParams(vmem_limit_bytes=VMEM_LIMIT),
        cost_estimate=pl.CostEstimate(flops=cost, bytes_accessed=1, transcendentals=0),
        name=name,
    )(info, *operands)


def whole(array):
    dims = array.shape
    return pl.BlockSpec(dims, lambda *_: (0,) * len(dims))


def dot(a, b):
    return jnp.dot(a, b, preferred_element_type=F32)


def dot_nt(a, b):
    return lax.dot_general(a, b, NT, preferred_element_type=F32)


def dot_tn(a, b):
    return lax.dot_general(a, b, TN, preferred_element_type=F32)


def hop(block, j):
    if not j:
        return block
    axes = tuple(name for name, bit in BITS if j & bit)
    last = 2 ** len(axes) - 1
    return lax.ppermute(block, axes, [(i, last - i) for i in range(last + 1)])


def ring_of(size):
    odd = [i for i in range(size) if i % 2 == 1]
    even = [i for i in range(size) if i % 2 == 0 and i > 0]
    return [0] + odd + even[::-1]


class Order:
    def __init__(self):
        self.gate = ()

    def do(self, function, info, *operands, **options):
        result = function(after(info, *self.gate), *operands, **options)
        self.gate = (jax.tree.leaves(result)[0],)
        return result

    def need(self, *moved):
        self.gate = self.gate + moved

    def then(self, value):
        return after(value, *self.gate) if self.gate else value


class Lane:
    def __init__(self, size):
        ring = ring_of(size)
        self.size = size
        self.route = [(ring[i], ring[(i + 1) % size]) for i in range(size)]
        self.last = ()

    def hop(self, block):
        if self.last:
            block = after(block, *self.last)
        moved = lax.ppermute(block, "z", self.route)
        self.last = (moved,)
        return moved

    def gather(self, block, steps=None):
        held = block if isinstance(block, list) else [block]
        for _ in range(steps or self.size - len(held)):
            held.append(self.hop(held[-1]))
        return held


class Sum:
    def __init__(self, order, lane, chunks):
        self.order, self.lane, self.total, self.rest = order, lane, chunks[0], list(chunks[1:])

    def move(self):
        if self.rest:
            moved = self.order.then(self.lane.hop(self.total)).astype(F32)
            self.total = (moved + self.rest.pop(0).astype(F32)).astype(BF16)
            self.order.need(self.total)

    def finish(self):
        while self.rest:
            self.move()


def near_parts(block, before_y=(), before_x=(), before_halves=()):
    half = block.shape[0] // 2
    from_y = hop(after(block, *before_y), 1)
    from_x = hop(after(block, *before_x), 2)
    first, second = after((from_y[:half], from_x[half:]), *before_halves)
    return [block, from_y, from_x, hop(first, 2), hop(second, 1)]


def join_kernel(cuts, info, *refs):
    count = len(cuts)
    out, sems = refs[count], refs[count + 1]
    copies, start = [], 0
    for i, (first, rows) in enumerate(cuts):
        source = refs[i].at[pl.ds(first, rows), :]
        copies.append(pltpu.make_async_copy(source, out.at[pl.ds(start, rows), :], sems.at[i]))
        start += rows
    for copy in copies:
        copy.start()
    for copy in copies:
        copy.wait()


def join(info, *blocks):
    blocks = [b if isinstance(b, tuple) else (b, 0, b.shape[0]) for b in blocks]
    arrays = [b[0] for b in blocks]
    cuts = tuple(b[1:] for b in blocks)
    out = shape((sum(rows for _, rows in cuts), arrays[0].shape[1]), arrays[0].dtype)
    anywhere = pl.BlockSpec(memory_space=pl.ANY)
    return call(
        functools.partial(join_kernel, cuts),
        info, (1,), [anywhere] * len(arrays), whole(out), out, arrays, "join", 0,
        [pltpu.SemaphoreType.DMA((len(arrays),))],
    )


def combine_kernel(info, near, moved, own, *outs):
    own[...] = near[0].astype(F32) + moved[0].astype(F32)
    for j, out in enumerate(outs):
        out[...] = (near[j + 1].astype(F32) + moved[j + 1].astype(F32)).astype(BF16)


def combine(info, near, moved):
    near = near.reshape(4, -1, near.shape[-1])
    moved = moved.reshape(near.shape)
    rows, columns = near.shape[1:]
    part = rows // 4
    outs = [shape((rows, columns), F32)] + [shape((rows, columns), BF16)] * 3
    source = pl.BlockSpec((4, part, columns), lambda i, s: (0, i, 0))
    return call(
        combine_kernel,
        info, (4,), [source, source], [pl.BlockSpec((part, columns), lambda i, s: (i, 0))] * 4,
        outs, (near, moved), "combine", 0,
    )


def near_moves(blocks):
    return [hop(block, j) for j, block in enumerate(blocks)]


def scatter_moves(own, *terms):
    return own, [hop(term, j + 1) for j, term in enumerate(terms)]


def meet_kernel(info, near, moved, *outs):
    rows = outs[0].shape[0] // 2
    for j, out in enumerate(outs):
        out[:rows, :] = near[j * rows : (j + 1) * rows, :]
        out[rows:, :] = moved[j * rows : (j + 1) * rows, :]


def meet(info, near, moved):
    outs = [shape((near.shape[0] // 2, near.shape[1]), near.dtype)] * 4
    return call(
        meet_kernel,
        info, (1,), [whole(near), whole(moved)], [whole(a) for a in outs], outs, (near, moved),
        "meet", 0,
    )


def pack_kernel(piece, width, info, weight_qkv, weight_out, gain, *outs):
    for k, j in enumerate(SHARD_TO_RANK):
        rank = jnp.bitwise_xor(info[RANK], j)
        for head in range(piece // HD):
            for part in range(3):
                start = pl.multiple_of(part * width + rank * piece + head * HD, HD)
                column = (head * 3 + part) * HD
                value = weight_qkv[:, pl.ds(start, HD)].astype(F32) * gain[...]
                outs[k][:, column : column + HD] = value.astype(BF16)
        outs[k][:, 3 * piece :] = weight_out[:, pl.ds(pl.multiple_of(rank * piece, piece), piece)]


def pack(info, weight_qkv, weight_out, gain):
    rows, width = weight_out.shape
    piece = width // 8
    outs = [shape((rows, 4 * piece), BF16)] * 4
    operands = (weight_qkv, weight_out, gain)
    return call(
        functools.partial(pack_kernel, piece, width),
        info, (1,), [whole(a) for a in operands], [whole(a) for a in outs], outs, operands,
        "pack", 0,
    )


def join_two_kernel(count, info, *refs):
    first, second = refs[count:]
    columns = first.shape[1]
    rows = refs[0].shape[0]
    for k in range(count):
        first[k * rows : (k + 1) * rows, :] = refs[k][:, :columns]
        second[k * rows : (k + 1) * rows, :] = refs[k][:, columns:]


def join_two(info, columns, *blocks):
    rows = sum(block.shape[0] for block in blocks)
    outs = [shape((rows, columns), BF16), shape((rows, blocks[0].shape[1] - columns), BF16)]
    return call(
        functools.partial(join_two_kernel, len(blocks)),
        info, (1,), [whole(a) for a in blocks], [whole(a) for a in outs], outs, blocks,
        "join_two", 0,
    )


def place_rows(info, parts, out):
    rows = parts[0].shape[0] // 4
    for s, source in enumerate(parts):
        for k in range(4):
            block = info[PLANES + s] * 4 + jnp.bitwise_xor(info[SHARD], k)
            out[pl.ds(pl.multiple_of(block * rows, rows), rows), :] = source[
                k * rows : (k + 1) * rows, :
            ]


def assemble_kernel(info, *refs):
    place_rows(info, refs[:-1], refs[-1])


def assemble(info, *parts):
    out = shape((len(parts) * parts[0].shape[0], parts[0].shape[1]), BF16)
    return call(
        assemble_kernel,
        info, (1,), [whole(a) for a in parts], whole(out), out, parts, "assemble", 0,
    )


def stack_kernel(count, cut, info, *refs):
    first, second = refs[count:]
    rest = refs[0].shape[0] - cut
    for s in range(count):
        plane = info[PLANES + s]
        first[pl.ds(pl.multiple_of(plane * cut, cut), cut), :] = refs[s][:cut, :]
        second[pl.ds(pl.multiple_of(plane * rest, rest), rest), :] = refs[s][cut:, :]
    for out, rows in ((first, cut), (second, rest)):
        if out.shape[0] > count * rows:
            out[count * rows :, :] = jnp.zeros((out.shape[0] - count * rows, out.shape[1]), BF16)


def stack_planes(info, cut, *parts):
    count, (rows, width) = len(parts), parts[0].shape
    outs = [
        shape((-(-count * size // 128) * 128, width), BF16) for size in (cut, rows - cut)
    ]
    return call(
        functools.partial(stack_kernel, count, cut),
        info, (1,), [whole(a) for a in parts], [whole(a) for a in outs], outs, parts, "stack", 0,
    )


def spread_kernel(count, rows, piece, info, *refs):
    out = refs[-1]
    for j in range(8):
        columns = pl.ds(
            pl.multiple_of(jnp.bitwise_xor(info[RANK], j) * piece, piece), piece
        )
        shift = 2 * ((j >> 1) & 1) + (j >> 2)
        source = refs[j // 4]
        base = (j % 4) * count * 4 * rows
        for s in range(count):
            for k in range(4):
                block = info[PLANES + s] * 4 + jnp.bitwise_xor(info[SHARD], k ^ shift)
                start = base + (s * 4 + k) * rows
                out[pl.ds(pl.multiple_of(block * rows, rows), rows), columns] = source[
                    start : start + rows, :
                ]


def spread(info, near, far, count):
    piece = near.shape[1]
    width = piece * 8
    rows = width // (4 * count)
    out = shape((width, width), BF16)
    return call(
        functools.partial(spread_kernel, count, rows, piece),
        info, (1,), [whole(near), whole(far)], whole(out), out, (near, far), "spread", 0,
    )


def project_kernel(count, info, near, far, *refs):
    parts, tables = refs[:count], refs[count : count + 4]
    weight, out, act_near, act_far = refs[count + 4 :]

    @pl.when(pl.program_id(0) == 0)
    def _():
        place_rows(info, parts, weight)

    for half, (tokens, act) in enumerate(((near, act_near), (far, act_far))):
        values = tokens[...].astype(F32)
        inverse = lax.rsqrt(jnp.mean(values * values, axis=1, keepdims=True) + EPS)
        act[...] = (values * inverse).astype(BF16)
        proj = dot(act[...], weight[...])
        for part in range(proj.shape[1] // HD):
            value = proj[:, part * HD : (part + 1) * HD]
            if part % 3 < 2:
                turned = pltpu.roll(value, HD // 2, 1)
                value = value * tables[half][...] + turned * tables[2 + half][...]
            out[half, :, part * HD : (part + 1) * HD] = value.astype(BF16)


def project(info, near, far, parts, cosine, sine):
    rows, width = near.shape
    tile = rows // 4
    columns = parts[0].shape[1]
    outs = [
        shape((width, columns), BF16),
        shape((2, rows, columns), BF16),
        shape((rows, width), BF16),
        shape((rows, width), BF16),
    ]
    tiles = pl.BlockSpec((tile, width), lambda i, s: (i, 0))
    first = pl.BlockSpec((tile, HD), lambda i, s: (i, 0))
    second = pl.BlockSpec((tile, HD), lambda i, s: (i + 4, 0))
    weight, out, act_near, act_far = call(
        functools.partial(project_kernel, len(parts)),
        info, (4,),
        [tiles, tiles]
        + [whole(a) for a in parts]
        + [first, second, first, second],
        [whole(outs[0]), pl.BlockSpec((2, tile, columns), lambda i, s: (0, i, 0)), tiles, tiles],
        outs, (near, far, *parts, cosine, cosine, sine, sine),
        "project", 4 * rows * width * columns,
    )
    return out.reshape(2 * rows, columns), weight, act_near, act_far


def place_of(block):
    return (block & 1) | ((block >> 1) & 1) << 2 | ((block >> 2) & 1) << 1


def lowest_key(block, rows, bound):
    pos = block * rows + lax.broadcasted_iota(jnp.int32, (rows, 1), 0)
    return jnp.maximum(jnp.where(pos >= bound, bound, 0), pos - (WINDOW - 1))


def block_scores(query, key, low, q_block, k_block, rows):
    scores = dot_nt(query, key) * HD**-0.5
    pos = k_block * rows + lax.broadcasted_iota(jnp.int32, (rows, rows), 1)
    seen = pos >= low
    if q_block == k_block:
        seen = seen & (
            lax.broadcasted_iota(jnp.int32, (rows, rows), 1)
            <= lax.broadcasted_iota(jnp.int32, (rows, rows), 0)
        )
    return jnp.where(seen, scores, NEG)


def key_blocks(q_block, rows):
    return range(max(0, q_block - WINDOW // rows), q_block + 1)


def row_start(block, rank, rows):
    return pl.multiple_of(jnp.bitwise_xor(place_of(block), rank) * rows, rows)


def attend_kernel(info, qkv, *refs):
    near, far, lse, result = refs
    rows = qkv.shape[0] // 8
    rank, bound = info[RANK], info[BOUND]
    for b in range(8):
        own = pl.ds(row_start(b, rank, rows), rows)
        query = qkv[own, :HD]
        low = lowest_key(b, rows, bound)
        spots = [(kb, pl.ds(row_start(kb, rank, rows), rows)) for kb in key_blocks(b, rows)]
        scores = [
            block_scores(query, qkv[at, HD : 2 * HD], low, b, kb, rows) for kb, at in spots
        ]
        top = functools.reduce(jnp.maximum, [jnp.max(s, axis=1, keepdims=True) for s in scores])
        powered = [jnp.exp(s - top) for s in scores]
        total = functools.reduce(jnp.add, [jnp.sum(p, axis=1, keepdims=True) for p in powered])
        inverse = 1.0 / total
        out = functools.reduce(
            jnp.add,
            [
                dot((p * inverse).astype(BF16), qkv[at, 2 * HD :])
                for p, (_, at) in zip(powered, spots)
            ],
        )
        result[own, :] = out.astype(BF16)
        lse[0, own, :] = top + jnp.log(total)
    near[...] = result[: 4 * rows, :]
    far[...] = result[4 * rows :, :]


def attend(info, qkv):
    length = qkv.shape[0]
    rows = length // 8
    heads = qkv.shape[1] // (3 * HD)
    outs = [shape((4 * rows, heads * HD), BF16)] * 2 + [shape((heads, length, 1), F32)]
    return call(
        attend_kernel,
        info, (heads,), [pl.BlockSpec((length, 3 * HD), lambda h, s: (0, h))],
        [pl.BlockSpec((4 * rows, HD), lambda h, s: (0, h))] * 2
        + [pl.BlockSpec((1, length, 1), lambda h, s: (h, 0, 0))],
        outs, (qkv,), "attend", 8 * heads * length * WINDOW * HD,
        [pltpu.VMEM((length, HD), BF16)],
    )


def attend_back_kernel(info, qkv, *refs):
    grads, (lse, cosine, sine, out, top_all, sum_key, sum_value) = refs[:4], refs[4:]
    rows = qkv.shape[0] // 8
    rank, bound = info[RANK], info[BOUND]
    sum_key[...] = jnp.zeros_like(sum_key)
    sum_value[...] = jnp.zeros_like(sum_value)
    for j in range(4):
        top_all[j * rows : (j + 1) * rows, :] = grads[j][:rows, :]
        top_all[(j + 4) * rows : (j + 5) * rows, :] = grads[j][rows:, :]

    def unturn(value, at):
        value = value.astype(BF16).astype(F32)
        turned = value * cosine[at, :] - pltpu.roll(value, HD // 2, 1) * sine[at, :]
        return turned.astype(BF16)

    for b in range(8):
        own = pl.ds(row_start(b, rank, rows), rows)
        query = qkv[own, :HD]
        top = top_all[own, :]
        low = lowest_key(b, rows, bound)
        log_total = lse[0, own, :]
        spots = [(kb, pl.ds(row_start(kb, rank, rows), rows)) for kb in key_blocks(b, rows)]
        probs = [
            jnp.exp(block_scores(query, qkv[at, HD : 2 * HD], low, b, kb, rows) - log_total)
            for kb, at in spots
        ]
        slopes = [dot_nt(top, qkv[at, 2 * HD :]) for _, at in spots]
        mean = functools.reduce(
            jnp.add, [jnp.sum(p * g, axis=1, keepdims=True) for p, g in zip(probs, slopes)]
        )
        sum_query = jnp.zeros((rows, HD), F32)
        for p, g, (_, at) in zip(probs, slopes, spots):
            low_grad = (p * (g - mean)).astype(BF16)
            sum_query = sum_query + dot(low_grad, qkv[at, HD : 2 * HD])
            sum_key[at, :] += dot_tn(low_grad, query)
            sum_value[at, :] += dot_tn(p.astype(BF16), top)
        out[own, :HD] = unturn(sum_query * HD**-0.5, own)

    @pl.loop(0, 8)
    def _(j):
        at = pl.ds(pl.multiple_of(j * rows, rows), rows)
        out[at, HD : 2 * HD] = unturn(sum_key[at, :] * HD**-0.5, at)
        out[at, 2 * HD :] = sum_value[at, :].astype(BF16)


def attend_back(info, qkv, grads, lse, cosine, sine, head):
    length = qkv.shape[0]
    rows = length // 8
    out = shape((length, 3 * HD), BF16)
    return call(
        attend_back_kernel,
        info, (1,),
        [pl.BlockSpec((length, 3 * HD), lambda i, s: (0, head))]
        + [pl.BlockSpec((2 * rows, HD), lambda i, s: (0, head))] * 4
        + [pl.BlockSpec((1, length, 1), lambda i, s: (head, 0, 0))]
        + [whole(cosine), whole(sine)],
        whole(out), out, (qkv, *grads, lse, cosine, sine), "attend_back",
        20 * length * WINDOW * HD,
        [
            pltpu.VMEM((length, HD), BF16),
            pltpu.VMEM((length, HD), F32),
            pltpu.VMEM((length, HD), F32),
        ],
    )


def branch_kernel(piece, info, *refs):
    blocks = refs[:4]
    weight, tokens, attn, middle, scale, act = refs[4:]
    step = pl.program_id(0)
    width = weight.shape[1]

    @pl.when(step == 0)
    def _():
        rows = tokens.shape[0]
        for j in range(8):
            start = pl.multiple_of(jnp.bitwise_xor(info[RANK], j) * piece, piece)
            first = j // 4 * rows
            attn[:, pl.ds(start, piece)] = blocks[j % 4][first : first + rows, :]

    at = pl.ds(pl.multiple_of(step * width, width), width)
    middle[:, at] = tokens[:, at].astype(F32) + dot(attn[...], weight[...])

    @pl.when(step == pl.num_programs(0) - 1)
    def _():
        value = middle[...]
        inverse = lax.rsqrt(jnp.mean(value * value, axis=1, keepdims=True) + EPS)
        scale[...] = inverse
        act[...] = (value * inverse).astype(BF16)


def branch(info, blocks, weight, tokens):
    rows, width = tokens.shape
    outs = [
        shape((rows, width), BF16),
        shape((rows, width), F32),
        shape((rows, 1), F32),
        shape((rows, width), BF16),
    ]
    return call(
        functools.partial(branch_kernel, width // 8),
        info, (4,),
        [whole(a) for a in blocks]
        + [pl.BlockSpec((width, width // 4), lambda i, s: (0, i)), whole(tokens)],
        [whole(a) for a in outs], outs, (*blocks, weight, tokens), "branch",
        2 * rows * width * width,
    )


def slopes_kernel(info, near, far, first, second, out_near, out_far):
    columns = first.shape[0]
    for top, out in ((near, out_near), (far, out_far)):
        out[:, :columns] = dot_nt(top[...], first[...])
        out[:, columns:] = dot_nt(top[...], second[...])


def slopes(info, near, far, first, second):
    rows, width = near.shape
    tile = rows // 4
    columns = first.shape[0] + second.shape[0]
    tiles = pl.BlockSpec((tile, width), lambda i, s: (i, 0))
    return call(
        slopes_kernel,
        info, (4,), [tiles, tiles, whole(first), whole(second)],
        [pl.BlockSpec((tile, columns), lambda i, s: (i, 0))] * 2,
        [shape((rows, columns), F32)] * 2, (near, far, first, second), "slopes",
        4 * rows * width * columns,
    )


def ffn_kernel(tail, more, info, *refs):
    if more:
        act, slope, pair, earlier, earlier_pair, hidden, grads, back = refs
    else:
        act, slope, pair, hidden, grads = refs
    double = pair.shape[1]
    main = double // 2 - tail
    proj = dot(act[...], pair[...])

    def gated(gate, up, grad):
        sigmoid = jax.nn.sigmoid(gate)
        silu = gate * sigmoid
        return (
            silu * up,
            grad * up * sigmoid * (1.0 + gate * (1.0 - sigmoid)),
            grad * silu,
        )

    value, to_gate, to_up = gated(proj[:, :main], proj[:, double - main :], slope[:, :main])
    hidden[:, :main] = value.astype(BF16)
    grads[:, :main] = to_gate.astype(BF16)
    grads[:, double - main :] = to_up.astype(BF16)
    if tail:
        mixed = proj[:, main : main + 2 * tail]
        value, to_gate, to_up = gated(
            mixed, pltpu.roll(mixed, tail, 1), slope[:, main : main + 2 * tail]
        )
        first = lax.broadcasted_iota(jnp.int32, mixed.shape, 1) < tail
        hidden[:, main : main + 2 * tail] = jnp.where(first, value, 0.0).astype(BF16)
        grads[:, main : main + 2 * tail] = jnp.where(
            first, to_gate, pltpu.roll(to_up, tail, 1)
        ).astype(BF16)
    if more:
        total = dot_nt(grads[...], pair[...]) + dot_nt(earlier[...], earlier_pair[...])
        back[...] = total.astype(BF16)


def ffn(info, act, slope, chunk, pair, earlier=None, earlier_pair=None):
    rows, width = act.shape
    tile = rows // 4
    double = pair.shape[1]
    columns = -(-double // 256) * 128
    offset = slope.shape[1] // columns - 1 if chunk else 0
    more = earlier is not None
    tiles = pl.BlockSpec((tile, width), lambda i, s: (i, 0))
    operands = [act, slope, pair]
    in_specs = [tiles, pl.BlockSpec((tile, columns), lambda i, s: (i, offset)), whole(pair)]
    outs = [shape((rows, columns), BF16), shape((rows, double), BF16)]
    out_specs = [
        pl.BlockSpec((tile, columns), lambda i, s: (i, 0)),
        pl.BlockSpec((tile, double), lambda i, s: (i, 0)),
    ]
    flops = 2 * rows * width * double
    if more:
        operands += [earlier, earlier_pair]
        in_specs += [
            pl.BlockSpec((tile, earlier.shape[1]), lambda i, s: (i, 0)),
            whole(earlier_pair),
        ]
        outs += [shape((rows, width), BF16)]
        out_specs += [tiles]
        flops += 2 * rows * width * (double + earlier.shape[1])
    return call(
        functools.partial(ffn_kernel, double // 2 % 128, more),
        info, (4,), in_specs, out_specs, outs, operands, "ffn", flops,
    )


def grad_rows_kernel(own_rows, info, act_near, act_far, near, far, *refs):
    outs, total = refs[:-1], refs[-1]
    total[...] = dot_tn(act_near[...], near[...]) + dot_tn(act_far[...], far[...])
    for i, out in enumerate(outs):

        @pl.when(pl.program_id(0) == i)
        def _():
            for k in range(4):
                start = jnp.bitwise_xor(info[SHARD], k) * own_rows
                value = total[pl.ds(pl.multiple_of(start, own_rows), own_rows), :]
                out[k * own_rows : (k + 1) * own_rows, :] = value.astype(BF16)


def grad_rows(info, act_near, act_far, near, far, count, name, split=False):
    rows, width = act_near.shape
    chunk = width // count
    columns = near.shape[1]

    def spot(i, s):
        return (0, s[PLANES + (i + 1) % count])

    acts = pl.BlockSpec((rows, chunk), spot)
    outs = [shape((chunk, columns), BF16)] * count
    first = pl.BlockSpec((rows, columns), lambda i, s: (0, 0))
    second = pl.BlockSpec((rows, columns), lambda i, s: (1 if split else 0, 0))
    return call(
        functools.partial(grad_rows_kernel, chunk // 4),
        info, (count,), [acts, acts, first, second], [whole(a) for a in outs], outs,
        (act_near, act_far, near, far), name, 4 * rows * width * columns,
        [pltpu.VMEM((chunk, columns), F32)],
    )


def grad_down_kernel(rows, info, first_near, first_far, second_near, second_far, *refs):
    top_near, top_far = refs[:2]
    outs, total = refs[2:-1], refs[-1]
    count = len(outs)
    start = 0
    for near, far, part in ((first_near, first_far, rows[0]), (second_near, second_far, rows[1])):
        units = near.shape[1]
        total[:units, :] = dot_tn(near[...], top_near[...]) + dot_tn(far[...], top_far[...])
        for i in range(count):
            at = pl.multiple_of(info[PLANES + (i + 1) % count] * part, part)
            outs[i][start : start + part, :] = total[pl.ds(at, part), :].astype(BF16)
        start += part


def grad_down(info, first, second, top_near, top_far, count, rows):
    tokens, width = top_near.shape
    part = width // 4
    outs = [shape((sum(rows), width), BF16)] * count
    tops = pl.BlockSpec((tokens, part), lambda i, s: (0, i))
    hidden = (*first, *second)
    units = max(a.shape[1] for a in hidden)
    return call(
        functools.partial(grad_down_kernel, rows),
        info, (4,), [whole(a) for a in hidden] + [tops, tops],
        [pl.BlockSpec((sum(rows), part), lambda i, s: (0, i))] * count, outs,
        (*hidden, top_near, top_far), "grad_down",
        4 * tokens * width * (first[0].shape[1] + second[0].shape[1]),
        [pltpu.VMEM((units, part), F32)],
    )


def matmul_two_kernel(info, a, b, c, d, out):
    out[...] = (dot(a[...], b[...]) + dot(c[...], d[...])).astype(BF16)


def down_product(info, first, second, down_first, down_second):
    rows, width = first.shape[0], down_first.shape[1]
    tile = rows // 4
    out = shape((rows, width), BF16)
    return call(
        matmul_two_kernel,
        info, (4,),
        [
            pl.BlockSpec((tile, first.shape[1]), lambda i, s: (i, 0)), whole(down_first),
            pl.BlockSpec((tile, second.shape[1]), lambda i, s: (i, 0)), whole(down_second),
        ],
        pl.BlockSpec((tile, width), lambda i, s: (i, 0)), out,
        (first, down_first, second, down_second), "down_product",
        2 * rows * width * (first.shape[1] + second.shape[1]),
    )


def grad_attn_kernel(info, *refs):
    own, first, second, third, top, middle, scale, weight = refs[:8]
    grad_middle, branch_ref, near, far = refs[8:]
    step = pl.program_id(0)
    rows = own.shape[0]

    @pl.when(step == 0)
    def _():
        grad = own[...]
        for moved in (first, second, third):
            grad = grad + moved[...].astype(F32)
        value, inverse = middle[...], scale[...]
        mean = jnp.mean(grad * value, axis=1, keepdims=True)
        total = top[...].astype(F32) + inverse * grad - value * (inverse**3 * mean)
        grad_middle[...] = total
        branch_ref[...] = total.astype(BF16)

    value = dot_nt(branch_ref[...], weight[...]).astype(BF16)
    for j in range(8):

        @pl.when(step == j)
        def _():
            out = far if j > 3 else near
            out[j % 4 * rows : (j % 4 + 1) * rows, :] = value


def grad_attn(info, own, parts, top, middle, scale, weight):
    rows, width = middle.shape
    piece = width // 8
    outs = [shape((rows, width), F32), shape((rows, width), BF16)]
    outs += [shape((4 * rows, piece), BF16)] * 2
    operands = (own, *parts, top, middle, scale)

    def spot(i, s):
        return (jnp.bitwise_xor(s[RANK], i), 0)

    return call(
        grad_attn_kernel,
        info, (8,), [whole(a) for a in operands] + [pl.BlockSpec((piece, width), spot)],
        [whole(a) for a in outs], outs, (*operands, weight), "grad_attn",
        2 * rows * width * width,
    )


def grad_out_kernel(info, attn, near_cols, far_cols, near, far):
    near[0] = dot_tn(attn[...], near_cols[...]).astype(BF16)
    far[0] = dot_tn(attn[...], far_cols[...]).astype(BF16)


def grad_out_terms(info, attn, grad):
    rows, width = attn.shape
    piece = width // 8
    outs = [shape((4, width, piece), BF16)] * 2
    return call(
        grad_out_kernel,
        info, (4,),
        [
            whole(attn),
            pl.BlockSpec((rows, piece), lambda i, s: (0, jnp.bitwise_xor(s[RANK], i))),
            pl.BlockSpec((rows, piece), lambda i, s: (0, jnp.bitwise_xor(s[RANK], i + 4))),
        ],
        [pl.BlockSpec((1, width, piece), lambda i, s: (i, 0, 0))] * 2, outs,
        (attn, grad, grad), "grad_out", 2 * rows * width * width,
    )


def order_kernel(own_rows, info, own, first, second, third, *refs):
    outs, total = refs[:-1], refs[-1]
    count = len(outs)
    value = own[...]
    for moved in (first, second, third):
        value = value + moved[...].astype(F32)
    total[...] = value
    for i, out in enumerate(outs):
        for k in range(4):
            block = info[PLANES + (i + 1) % count] * 4 + jnp.bitwise_xor(info[SHARD], k)
            value = total[pl.ds(pl.multiple_of(block * own_rows, own_rows), own_rows), :]
            out[k * own_rows : (k + 1) * own_rows, :] = value.astype(BF16)


def order_out(info, own, parts, count):
    width, columns = own.shape
    outs = [shape((width // count, columns), BF16)] * count
    return call(
        functools.partial(order_kernel, width // count // 4),
        info, (1,), [whole(a) for a in (own, *parts)], [whole(a) for a in outs], outs,
        (own, *parts), "order_out", 0, [pltpu.VMEM((width, columns), F32)],
    )


def back_product_kernel(info, first, second, weight, out):
    columns = first.shape[1]
    total = dot_nt(first[...], weight[:, :columns]) + dot_nt(second[...], weight[:, columns:])
    out[...] = total.astype(BF16)


def back_product(info, first, second, weight, far):
    rows, width = first.shape[0] // 2, weight.shape[0]
    tile = rows // 4
    out = shape((rows, width), BF16)
    tiles = pl.BlockSpec((tile, first.shape[1]), lambda i, s: (i + (4 if far else 0), 0))
    return call(
        back_product_kernel,
        info, (4,), [tiles, tiles, whole(weight)],
        pl.BlockSpec((tile, width), lambda i, s: (i, 0)), out, (first, second, weight),
        "back_product", 2 * rows * width * weight.shape[1],
    )


def rank_block(info, j, mine, theirs):
    rows = mine.shape[0] // 4
    source = theirs if j % 2 else mine
    return source[j // 2 * rows : (j // 2 + 1) * rows, :]


def finish_qkv_kernel(info, *refs):
    pairs = (refs[:2], refs[2:4])
    weight, gain, out, gain_out = refs[4:]
    rows, width = out.shape[0], out.shape[1] // 3
    total = jnp.zeros((rows, HD), F32)
    for j in range(8):
        rank = jnp.bitwise_xor(info[RANK], j)
        for head, pair in enumerate(pairs):
            block = rank_block(info, j, *pair)
            for part in range(3):
                start = pl.multiple_of(part * width + (2 * rank + head) * HD, HD)
                value = block[:, part * HD : (part + 1) * HD].astype(F32)
                out[:, pl.ds(start, HD)] = value * gain[...]
                total = total + value * weight[:, pl.ds(start, HD)].astype(F32)
    gain_out[...] = jnp.sum(total, axis=1, keepdims=True)


def finish_qkv(info, first, second, weight, gain):
    outs = [shape(weight.shape, F32), shape(gain.shape, F32)]
    operands = (*first, *second, weight, gain)
    return call(
        finish_qkv_kernel,
        info, (1,), [whole(a) for a in operands], [whole(a) for a in outs], outs, operands,
        "finish_qkv", 0,
    )


def finish_out_kernel(info, mine, theirs, out):
    piece = mine.shape[1]
    for j in range(8):
        start = pl.multiple_of(jnp.bitwise_xor(info[RANK], j) * piece, piece)
        out[:, pl.ds(start, piece)] = rank_block(info, j, mine, theirs).astype(F32)


def finish_out(info, mine, theirs):
    rows, piece = mine.shape[0] // 4, mine.shape[1]
    out = shape((rows, 8 * piece), F32)
    return call(
        finish_out_kernel,
        info, (1,), [whole(mine), whole(theirs)], whole(out), out, (mine, theirs),
        "finish_out", 0,
    )


def unit_lanes(first, count, local):
    main = local // 128 * 128
    runs = []
    while count:
        size = min(count, main - first) if first < main else count
        up = local + (local - main) + first if first < main else local + first - main
        runs.append((first, up, size))
        first, count = first + size, count - size
    return runs


def finish_pair_kernel(planes, reals, pads, info, *refs):
    chunks = (refs[:2], refs[2:4])
    weights, gain, outs, gain_out = refs[4:6], refs[6], refs[7:9], refs[9]
    held = refs[10:]
    rows, width = outs[0].shape
    half_down = sum(reals)
    for (mine, theirs), by_rank in zip(chunks, held):
        for j in range(8):
            start = jnp.bitwise_xor(info[RANK], j) * rows
            block = rank_block(info, j, mine, theirs)
            by_rank[pl.ds(pl.multiple_of(start, rows), rows), :] = block[...].astype(F32)

    def move(chunk, rank, lane, out, column, size):
        source, target = lane // 128 * 128, column // 128 * 128
        wide = 128 if (lane - source) + size <= 128 and (column - target) + size <= 128 else 256
        at = slice(rank * rows, (rank + 1) * rows)
        if (lane - source) + size <= 128:
            value = held[chunk][at, source : source + 128]
            if wide == 256:
                value = jnp.concatenate([value, value], axis=1)
        else:
            value = held[chunk][at, source : source + 256]
        shift = ((column - target) - (lane - source)) % wide
        if shift:
            value = pltpu.roll(value, shift, 1)
        lanes = lax.broadcasted_iota(jnp.int32, value.shape, 1)
        keep = (lanes >= column - target) & (lanes < column - target + size)
        spot = slice(target, min(target + wide, width))
        if target + wide > width:
            value, keep = value[:, : width - target], keep[:, : width - target]
        out[:, spot] = jnp.where(keep, value, out[:, spot])

    for plane in range(planes):
        for rank in range(8):
            shard = 2 * (rank >> 1 & 1) + (rank >> 2)
            column = ((plane * 4 + shard) * 2 + (rank & 1)) * half_down
            for chunk, (real, pad) in enumerate(zip(reals, pads)):
                start = column
                for gate, up, size in unit_lanes(plane * pad, real, planes * pad):
                    move(chunk, rank, gate, outs[0], start, size)
                    move(chunk, rank, up, outs[1], start, size)
                    start += size
                column += real
    total = jnp.zeros((rows, 128), F32)
    for weight, out in zip(weights, outs):
        for tile in range(width // 128):
            at = slice(tile * 128, (tile + 1) * 128)
            value = out[:, at]
            total = total + value * weight[:, at].astype(F32)
            out[:, at] = value * gain[...]
    gain_out[...] = jnp.sum(total, axis=1, keepdims=True)


def finish_pair(info, first, second, gate, up, gain, planes, reals, pads):
    rows = gate.shape[0]
    outs = [shape(gate.shape, F32)] * 2 + [shape(gain.shape, F32)]
    operands = (*first, *second, gate, up, gain)
    return call(
        functools.partial(finish_pair_kernel, planes, reals, pads),
        info, (1,), [whole(a) for a in operands], [whole(a) for a in outs], outs, operands,
        "finish_pair", 0,
        [pltpu.VMEM((8 * rows, pair[0].shape[1]), F32) for pair in (first, second)],
    )


def on_device(
    planes,
    tokens,
    bounds,
    norm_attn,
    weight_qkv,
    weight_out,
    norm_ffn,
    weight_gate,
    weight_up,
    weight_down,
    cotangent,
):
    rows, width = tokens.shape[1], tokens.shape[2]
    own_rows = weight_qkv.shape[0]
    half_down = weight_down.shape[0] // 2
    cut = -(-half_down // 32) * 16
    pads = (cut, -(-(half_down - cut) // 16) * 16)
    reals = (cut, half_down - cut)
    starts = (0, cut)

    y, z, x, c = (lax.axis_index(name) for name in ("y", "z", "x", "c"))
    rank = 4 * c + 2 * x + y
    shard = 2 * x + c
    ring_list = ring_of(planes)
    table = [
        [ring_list[(ring_list.index(i) - s) % planes] for s in range(planes)]
        for i in range(planes)
    ]
    arrival = jnp.asarray(table, jnp.int32)[z]
    boundary = lax.dynamic_index_in_dim(bounds, z, 0, False)
    info = jnp.concatenate([jnp.stack([rank, boundary, shard]).astype(jnp.int32), arrival])
    order = Order()
    do, need = order.do, order.need
    lane_a, lane_b = Lane(planes), Lane(planes)

    def spread_pieces(pieces):
        return [hop(piece, j) for piece, j in zip(pieces, SHARD_TO_RANK)]

    def owners(total):
        return [
            hop(total[k * own_rows : (k + 1) * own_rows], SHARD_TO_RANK[k]) for k in (2, 1, 3)
        ]

    def rows_of(total, pieces):
        need(*pieces)
        mine = do(join, info, (total, 0, own_rows), *pieces)
        return mine, hop(mine, 1)

    down_own = lax.dynamic_slice_in_dim(weight_down, y * half_down, half_down, 0)
    down_own = jnp.pad(down_own, [(0, sum(pads) - half_down), (0, 0)])
    down_got = lane_a.gather(down_own, 1)
    wide_attn = norm_attn.astype(F32)[:, None]
    wide_ffn = norm_ffn.astype(F32)[:, None]
    pieces = spread_pieces(do(pack, info, weight_qkv, weight_out, wide_attn))
    token_parts = near_parts(tokens[0], (), pieces[1:])

    def split_hidden(weight):
        split = (after(weight, *pieces).astype(F32) * wide_ffn).astype(BF16)
        split = split.reshape(own_rows, planes, 2, 2, 2, half_down)
        return split.transpose(3, 2, 4, 0, 1, 5).reshape(8, own_rows, planes, half_down)

    gate_split, up_split = split_hidden(weight_gate), split_hidden(weight_up)
    pair_pieces = []
    for start, real, pad in zip(starts, reals, pads):
        both = []
        for split in (gate_split, up_split):
            part = split[..., start : start + real]
            part = jnp.pad(part, [(0, 0)] * 3 + [(0, pad - real)])
            both.append(part.reshape(8, own_rows, planes * pad))
        main = planes * pad // 128 * 128
        pair_pieces += [both[0], both[1][..., main:], both[1][..., :main]]
    pair_pieces = jnp.concatenate(pair_pieces, axis=-1)
    pair_pieces = spread_pieces(
        [
            lax.dynamic_index_in_dim(pair_pieces, jnp.bitwise_xor(rank, j), 0, False)
            for j in SHARD_TO_RANK
        ]
    )

    blocks = jnp.asarray([place_of(i) for i in range(8)], jnp.int32)
    blocks = jnp.take(blocks, jnp.bitwise_xor(jnp.arange(8, dtype=jnp.int32), rank))
    positions = (blocks[:, None] * rows + jnp.arange(rows, dtype=jnp.int32)[None, :]).reshape(-1)
    frequency = THETA ** (-jnp.arange(HD // 2, dtype=F32) * 2.0 / HD)
    angles = positions.astype(F32)[:, None] * frequency[None, :]
    cosine = jnp.cos(angles)
    sine = jnp.sin(angles)
    cosine = jnp.concatenate([cosine, cosine], axis=1)
    sine = jnp.concatenate([-sine, sine], axis=1)

    need(down_got[1], *pieces[1:])
    qkv_plane, out_plane = do(join_two, info, 3 * (width // 8), *pieces)
    out_got = lane_b.gather(out_plane)
    qkv_got = lane_b.gather(qkv_plane)
    need(*out_got)
    out_cols = do(join, info, *out_got)
    need(qkv_got[1], *pair_pieces[1:])
    pair_first, pair_second = do(join_two, info, 2 * planes * pads[0], *pair_pieces)
    out_parts = near_parts(out_cols, token_parts[1:2], pair_pieces, token_parts)
    need(*token_parts, qkv_got[2])
    tokens_near = do(join, info, *token_parts)
    tokens_far = hop(tokens_near, 4)
    lane_a.last = (qkv_got[-1],)
    pair_first_got = lane_b.gather(pair_first)
    down_got = lane_a.gather(down_got)
    pair_second_got = lane_a.gather(pair_second)
    need(tokens_far, *qkv_got)
    qkv, full_qkv, act_near, act_far = do(
        project, info, tokens_near, tokens_far, qkv_got, cosine, sine
    )
    need(*out_parts, down_got[2], pair_first_got[1])
    out_near = do(join, info, *out_parts)
    out_far = hop(out_near, 4)
    top_parts = near_parts(after(cotangent[0], *out_parts))
    attn_near, attn_far, lse = do(attend, info, qkv)
    moved = hop(attn_far, 4)
    need(out_far)
    full_out = do(spread, info, out_near, out_far, planes)
    need(moved, pair_first_got[2])
    attn_moved = near_moves(do(meet, info, attn_near, moved))
    need(*attn_moved)
    attn, middle, scale, act_own = do(branch, info, attn_moved, full_out, tokens[0])
    act_parts = near_parts(act_own)
    need(*top_parts, *down_got)
    top_near = do(join, info, *top_parts)
    top_far = hop(top_near, 4)
    need(*pair_first_got)
    down_a, down_b = do(stack_planes, info, pads[0], *down_got)
    need(top_far)
    slope_near, slope_far = do(slopes, info, top_near, top_far, down_a, down_b)
    full_first = do(assemble, info, *pair_first_got)
    need(*act_parts, pair_second_got[1])
    ffn_near = do(join, info, *act_parts)
    ffn_far = hop(ffn_near, 4)

    hidden_near, grads_near = do(ffn, info, ffn_near, slope_near, 0, full_first)
    need(ffn_far, pair_second_got[2])
    hidden_far, grads_far = do(ffn, info, ffn_far, slope_far, 0, full_first)
    lane_c = Lane(planes)
    pair_a = Sum(
        order,
        lane_b,
        do(grad_rows, info, ffn_near, ffn_far, grads_near, grads_far, planes, "grad_pair"),
    )
    need(*pair_second_got)
    full_second = do(assemble, info, *pair_second_got)
    second_far, more_far, far_terms = do(
        ffn, info, ffn_far, slope_far, 1, full_second, grads_far, full_first
    )
    moved = hop(far_terms, 4)
    second_near, more_near, near_terms = do(
        ffn, info, ffn_near, slope_near, 1, full_second, grads_near, full_first
    )
    pair_a.move()
    need(moved)
    own, parts = scatter_moves(*do(combine, info, near_terms, moved))
    pair_b = Sum(
        order,
        lane_a,
        do(grad_rows, info, ffn_near, ffn_far, more_near, more_far, planes, "grad_pair"),
    )
    pair_a.move()
    down_sum = Sum(
        order,
        lane_b,
        do(
            grad_down, info, (hidden_near, hidden_far), (second_near, second_far),
            top_near, top_far, planes, pads,
        ),
    )
    block_near = do(down_product, info, hidden_near, second_near, down_a, down_b)
    need(*parts)

    grad_middle, grad_branch, attn_near, attn_far = do(
        grad_attn, info, own, parts, cotangent[0], middle, scale, full_out
    )
    pair_a.move()
    away = hop(attn_far, 4)
    near_out, far_out = do(grad_out_terms, info, attn, grad_branch)
    pair_b.move()
    first_pieces = owners(pair_a.total)
    need(away)
    attn_grads = near_moves(do(meet, info, attn_near, away))
    out_moved = hop(after(far_out, attn_grads[0]), 4)
    need(*first_pieces)
    block_far = do(down_product, info, hidden_far, second_far, down_a, down_b)
    need(*attn_grads)
    grads_first = do(attend_back, info, qkv, attn_grads, lse, cosine, sine, 0)
    pair_b.move()
    sums_first = rows_of(pair_a.total, first_pieces)
    need(out_moved)
    out_own, out_parts = scatter_moves(*do(combine, info, near_out, out_moved))
    down_sum.move()
    qkv_first = Sum(
        order,
        lane_a,
        do(grad_rows, info, act_near, act_far, grads_first, grads_first, planes, "grad_qkv", True),
    )
    block_moved = hop(after(block_far, qkv_first.total), 4)
    grads_second = do(attend_back, info, qkv, attn_grads, lse, cosine, sine, 1)
    pair_b.move()
    second_pieces = owners(after(pair_b.total, *out_parts))
    down_sum.move()
    need(block_moved)
    block_terms = do(combine, info, block_near, block_moved)
    qkv_first.move()
    need(*out_parts)
    qkv_second = Sum(
        order,
        lane_b,
        do(
            grad_rows, info, act_near, act_far, grads_second, grads_second, planes,
            "grad_qkv", True,
        ),
    )
    block_own, block_parts = scatter_moves(block_terms[0], *after(block_terms[1:], *out_parts))
    down_sum.move()

    in_far = do(back_product, info, grads_first, grads_second, full_qkv, True)
    in_moved = hop(in_far, 4)
    qkv_first.move()
    down_mine = down_sum.total[:half_down]
    down_theirs = hop(down_mine, 1)
    in_near = do(back_product, info, grads_first, grads_second, full_qkv, False)
    out_sum = Sum(order, lane_c, do(order_out, info, out_own, out_parts, planes))
    sums_second = rows_of(pair_b.total, second_pieces)
    qkv_second.move()
    need(in_moved)
    in_own, in_parts = scatter_moves(*do(combine, info, in_near, in_moved))
    qkv_first.move()
    out_sum.move()
    need(*sums_first, *sums_second, *block_parts)
    sum_gate, sum_up, gain_sum_ffn = do(
        finish_pair, info, sums_first, sums_second, weight_gate, weight_up, wide_ffn,
        planes, reals, pads,
    )
    first_pieces = owners(qkv_first.total)
    qkv_second.move()
    out_sum.finish()
    need(*in_parts)
    first_rows = rows_of(qkv_first.total, first_pieces)
    out_pieces = owners(out_sum.total)
    qkv_second.finish()
    second_pieces = owners(qkv_second.total)
    out_rows = rows_of(out_sum.total, out_pieces)
    second_rows = rows_of(qkv_second.total, second_pieces)

    down_both = jnp.stack([down_mine, down_theirs])
    sum_down = jnp.concatenate(
        [lax.dynamic_index_in_dim(down_both, jnp.bitwise_xor(y, i), 0, False) for i in range(2)]
    ).astype(F32)
    need(out_rows[1])
    sum_out = do(finish_out, info, *out_rows)
    need(first_rows[1], second_rows[1])
    sum_qkv, gain_sum_attn = do(
        finish_qkv, info, first_rows, second_rows, weight_qkv, wide_attn
    )
    block_out = middle + block_own + sum(part.astype(F32) for part in block_parts)
    inputs = tokens[0].astype(F32)
    inv_attn = lax.rsqrt(jnp.mean(inputs * inputs, axis=-1, keepdims=True) + EPS)
    scaled = in_own + sum(part.astype(F32) for part in in_parts)
    grad_tokens = (
        grad_middle
        + inv_attn * scaled
        - inputs * inv_attn**3 * jnp.mean(scaled * inputs, axis=-1, keepdims=True)
    )
    return (
        block_out.astype(BF16)[None],
        grad_tokens[None],
        gain_sum_attn[:, 0],
        sum_qkv,
        sum_out,
        gain_sum_ffn[:, 0],
        sum_gate,
        sum_up,
        sum_down,
    )


def solution(mesh):
    planes = mesh.shape["fsdp"] // 4
    grid = Mesh(mesh.devices.reshape(2, planes, 2, 2), ("y", "z", "x", "c"))
    fsdp = ("z", "x", "c")
    by_token = P(fsdp, "y", None)
    by_row = P(fsdp, None)
    gain = P(fsdp)
    return jax.shard_map(
        functools.partial(on_device, planes),
        mesh=grid,
        in_specs=(
            by_token, P(), gain, by_row, by_row, gain, by_row, by_row, by_row, by_token,
        ),
        out_specs=(
            by_token, by_token, gain, by_row, by_row, gain, by_row, by_row, by_row,
        ),
        check_vma=False,
    )
```

```python
import functools

import jax
import jax.numpy as jnp
from jax import lax
from jax.experimental import pallas as pl
from jax.experimental.pallas import tpu as pltpu
from jax.sharding import Mesh, PartitionSpec as P

HD = 128
WINDOW = 1024
EPS = 1e-05
NEG = -1e30
THETA = 10000.0
F32 = jnp.float32
BF16 = jnp.bfloat16
BITS = (("y", 1), ("x", 2), ("c", 4))
SHARD_TO_RANK = (0, 4, 2, 6)
NT = (((1,), (1,)), ((), ()))
TN = (((0,), (0,)), ((), ()))
VMEM_LIMIT = 56 * 2**20
RANK, BOUND, SHARD, PLANES = 0, 1, 2, 3


def shape(dims, dtype):
    return jax.ShapeDtypeStruct(tuple(dims), dtype)


def after(value, *earlier):
    return lax.optimization_barrier((value, *earlier))[0]


def call(kernel, info, grid, in_specs, out_specs, out_shape, operands, name, flops, scratch=()):
    traffic = sum(a.size * a.dtype.itemsize for a in operands)
    traffic += sum(s.size * s.dtype.itemsize for s in jax.tree.leaves(out_shape))
    cost = int(1.2e9 + 230 * traffic)
    return pl.pallas_call(
        kernel,
        grid_spec=pltpu.PrefetchScalarGridSpec(
            num_scalar_prefetch=1,
            grid=grid,
            in_specs=in_specs,
            out_specs=out_specs,
            scratch_shapes=scratch,
        ),
        out_shape=out_shape,
        compiler_params=pltpu.CompilerParams(vmem_limit_bytes=VMEM_LIMIT),
        cost_estimate=pl.CostEstimate(flops=cost, bytes_accessed=1, transcendentals=0),
        name=name,
    )(info, *operands)


def whole(array):
    dims = array.shape
    return pl.BlockSpec(dims, lambda *_: (0,) * len(dims))


def dot(a, b):
    return jnp.dot(a, b, preferred_element_type=F32)


def dot_nt(a, b):
    return lax.dot_general(a, b, NT, preferred_element_type=F32)


def dot_tn(a, b):
    return lax.dot_general(a, b, TN, preferred_element_type=F32)


def hop(block, j):
    if not j:
        return block
    axes = tuple(name for name, bit in BITS if j & bit)
    last = 2 ** len(axes) - 1
    return lax.ppermute(block, axes, [(i, last - i) for i in range(last + 1)])


def ring_of(size):
    odd = [i for i in range(size) if i % 2 == 1]
    even = [i for i in range(size) if i % 2 == 0 and i > 0]
    return [0] + odd + even[::-1]


class Order:
    def __init__(self):
        self.gate = ()

    def do(self, function, info, *operands, **options):
        result = function(after(info, *self.gate), *operands, **options)
        self.gate = (jax.tree.leaves(result)[0],)
        return result

    def need(self, *moved):
        self.gate = self.gate + moved

    def then(self, value):
        return after(value, *self.gate) if self.gate else value


class Lane:
    def __init__(self, size):
        ring = ring_of(size)
        self.size = size
        self.route = [(ring[i], ring[(i + 1) % size]) for i in range(size)]
        self.last = ()

    def hop(self, block):
        if self.last:
            block = after(block, *self.last)
        moved = lax.ppermute(block, "z", self.route)
        self.last = (moved,)
        return moved

    def gather(self, block, steps=None):
        held = block if isinstance(block, list) else [block]
        for _ in range(steps or self.size - len(held)):
            held.append(self.hop(held[-1]))
        return held


class Sum:
    def __init__(self, order, lane, chunks):
        self.order, self.lane, self.total, self.rest = order, lane, chunks[0], list(chunks[1:])

    def move(self):
        if self.rest:
            moved = self.order.then(self.lane.hop(self.total)).astype(F32)
            self.total = (moved + self.rest.pop(0).astype(F32)).astype(BF16)
            self.order.need(self.total)

    def finish(self):
        while self.rest:
            self.move()


def near_parts(block, before_y=(), before_x=(), before_halves=()):
    half = block.shape[0] // 2
    from_y = hop(after(block, *before_y), 1)
    from_x = hop(after(block, *before_x), 2)
    first, second = after((from_y[:half], from_x[half:]), *before_halves)
    return [block, from_y, from_x, hop(first, 2), hop(second, 1)]


def join_kernel(cuts, info, *refs):
    count = len(cuts)
    out, sems = refs[count], refs[count + 1]
    copies, start = [], 0
    for i, (first, rows) in enumerate(cuts):
        source = refs[i].at[pl.ds(first, rows), :]
        copies.append(pltpu.make_async_copy(source, out.at[pl.ds(start, rows), :], sems.at[i]))
        start += rows
    for copy in copies:
        copy.start()
    for copy in copies:
        copy.wait()


def join(info, *blocks):
    blocks = [b if isinstance(b, tuple) else (b, 0, b.shape[0]) for b in blocks]
    arrays = [b[0] for b in blocks]
    cuts = tuple(b[1:] for b in blocks)
    out = shape((sum(rows for _, rows in cuts), arrays[0].shape[1]), arrays[0].dtype)
    anywhere = pl.BlockSpec(memory_space=pl.ANY)
    return call(
        functools.partial(join_kernel, cuts),
        info, (1,), [anywhere] * len(arrays), whole(out), out, arrays, "join", 0,
        [pltpu.SemaphoreType.DMA((len(arrays),))],
    )


def combine_kernel(info, near, moved, own, *outs):
    own[...] = near[0].astype(F32) + moved[0].astype(F32)
    for j, out in enumerate(outs):
        out[...] = (near[j + 1].astype(F32) + moved[j + 1].astype(F32)).astype(BF16)


def combine(info, near, moved):
    near = near.reshape(4, -1, near.shape[-1])
    moved = moved.reshape(near.shape)
    rows, columns = near.shape[1:]
    part = rows // 4
    outs = [shape((rows, columns), F32)] + [shape((rows, columns), BF16)] * 3
    source = pl.BlockSpec((4, part, columns), lambda i, s: (0, i, 0))
    return call(
        combine_kernel,
        info, (4,), [source, source], [pl.BlockSpec((part, columns), lambda i, s: (i, 0))] * 4,
        outs, (near, moved), "combine", 0,
    )


def near_moves(blocks):
    return [hop(block, j) for j, block in enumerate(blocks)]


def scatter_moves(own, *terms):
    return own, [hop(term, j + 1) for j, term in enumerate(terms)]


def meet_kernel(info, near, moved, *outs):
    rows = outs[0].shape[0] // 2
    for j, out in enumerate(outs):
        out[:rows, :] = near[j * rows : (j + 1) * rows, :]
        out[rows:, :] = moved[j * rows : (j + 1) * rows, :]


def meet(info, near, moved):
    outs = [shape((near.shape[0] // 2, near.shape[1]), near.dtype)] * 4
    return call(
        meet_kernel,
        info, (1,), [whole(near), whole(moved)], [whole(a) for a in outs], outs, (near, moved),
        "meet", 0,
    )


def pack_kernel(piece, width, info, weight_qkv, weight_out, gain, *outs):
    for k, j in enumerate(SHARD_TO_RANK):
        rank = jnp.bitwise_xor(info[RANK], j)
        for head in range(piece // HD):
            for part in range(3):
                start = pl.multiple_of(part * width + rank * piece + head * HD, HD)
                column = (head * 3 + part) * HD
                value = weight_qkv[:, pl.ds(start, HD)].astype(F32) * gain[...]
                outs[k][:, column : column + HD] = value.astype(BF16)
        outs[k][:, 3 * piece :] = weight_out[:, pl.ds(pl.multiple_of(rank * piece, piece), piece)]


def pack(info, weight_qkv, weight_out, gain):
    rows, width = weight_out.shape
    piece = width // 8
    outs = [shape((rows, 4 * piece), BF16)] * 4
    operands = (weight_qkv, weight_out, gain)
    return call(
        functools.partial(pack_kernel, piece, width),
        info, (1,), [whole(a) for a in operands], [whole(a) for a in outs], outs, operands,
        "pack", 0,
    )


def join_two_kernel(count, info, *refs):
    first, second = refs[count:]
    columns = first.shape[1]
    rows = refs[0].shape[0]
    for k in range(count):
        first[k * rows : (k + 1) * rows, :] = refs[k][:, :columns]
        second[k * rows : (k + 1) * rows, :] = refs[k][:, columns:]


def join_two(info, columns, *blocks):
    rows = sum(block.shape[0] for block in blocks)
    outs = [shape((rows, columns), BF16), shape((rows, blocks[0].shape[1] - columns), BF16)]
    return call(
        functools.partial(join_two_kernel, len(blocks)),
        info, (1,), [whole(a) for a in blocks], [whole(a) for a in outs], outs, blocks,
        "join_two", 0,
    )


def place_rows(info, parts, out):
    rows = parts[0].shape[0] // 4
    for s, source in enumerate(parts):
        for k in range(4):
            block = info[PLANES + s] * 4 + jnp.bitwise_xor(info[SHARD], k)
            out[pl.ds(pl.multiple_of(block * rows, rows), rows), :] = source[
                k * rows : (k + 1) * rows, :
            ]


def assemble_kernel(info, *refs):
    place_rows(info, refs[:-1], refs[-1])


def assemble(info, *parts):
    out = shape((len(parts) * parts[0].shape[0], parts[0].shape[1]), BF16)
    return call(
        assemble_kernel,
        info, (1,), [whole(a) for a in parts], whole(out), out, parts, "assemble", 0,
    )


def stack_kernel(count, cut, info, *refs):
    first, second = refs[count:]
    rest = refs[0].shape[0] - cut
    for s in range(count):
        plane = info[PLANES + s]
        first[pl.ds(pl.multiple_of(plane * cut, cut), cut), :] = refs[s][:cut, :]
        second[pl.ds(pl.multiple_of(plane * rest, rest), rest), :] = refs[s][cut:, :]
    for out, rows in ((first, cut), (second, rest)):
        if out.shape[0] > count * rows:
            out[count * rows :, :] = jnp.zeros((out.shape[0] - count * rows, out.shape[1]), BF16)


def stack_planes(info, cut, *parts):
    count, (rows, width) = len(parts), parts[0].shape
    outs = [
        shape((-(-count * size // 128) * 128, width), BF16) for size in (cut, rows - cut)
    ]
    return call(
        functools.partial(stack_kernel, count, cut),
        info, (1,), [whole(a) for a in parts], [whole(a) for a in outs], outs, parts, "stack", 0,
    )


def spread_kernel(count, rows, piece, info, *refs):
    out = refs[-1]
    for j in range(8):
        columns = pl.ds(
            pl.multiple_of(jnp.bitwise_xor(info[RANK], j) * piece, piece), piece
        )
        shift = 2 * ((j >> 1) & 1) + (j >> 2)
        source = refs[j // 4]
        base = (j % 4) * count * 4 * rows
        for s in range(count):
            for k in range(4):
                block = info[PLANES + s] * 4 + jnp.bitwise_xor(info[SHARD], k ^ shift)
                start = base + (s * 4 + k) * rows
                out[pl.ds(pl.multiple_of(block * rows, rows), rows), columns] = source[
                    start : start + rows, :
                ]


def spread(info, near, far, count):
    piece = near.shape[1]
    width = piece * 8
    rows = width // (4 * count)
    out = shape((width, width), BF16)
    return call(
        functools.partial(spread_kernel, count, rows, piece),
        info, (1,), [whole(near), whole(far)], whole(out), out, (near, far), "spread", 0,
    )


def project_kernel(count, info, near, far, *refs):
    parts, tables = refs[:count], refs[count : count + 4]
    weight, out, act_near, act_far = refs[count + 4 :]

    @pl.when(pl.program_id(0) == 0)
    def _():
        place_rows(info, parts, weight)

    for half, (tokens, act) in enumerate(((near, act_near), (far, act_far))):
        values = tokens[...].astype(F32)
        inverse = lax.rsqrt(jnp.mean(values * values, axis=1, keepdims=True) + EPS)
        act[...] = (values * inverse).astype(BF16)
        proj = dot(act[...], weight[...])
        for part in range(proj.shape[1] // HD):
            value = proj[:, part * HD : (part + 1) * HD]
            if part % 3 < 2:
                turned = pltpu.roll(value, HD // 2, 1)
                value = value * tables[half][...] + turned * tables[2 + half][...]
            out[half, :, part * HD : (part + 1) * HD] = value.astype(BF16)


def project(info, near, far, parts, cosine, sine):
    rows, width = near.shape
    tile = rows // 4
    columns = parts[0].shape[1]
    outs = [
        shape((width, columns), BF16),
        shape((2, rows, columns), BF16),
        shape((rows, width), BF16),
        shape((rows, width), BF16),
    ]
    tiles = pl.BlockSpec((tile, width), lambda i, s: (i, 0))
    first = pl.BlockSpec((tile, HD), lambda i, s: (i, 0))
    second = pl.BlockSpec((tile, HD), lambda i, s: (i + 4, 0))
    weight, out, act_near, act_far = call(
        functools.partial(project_kernel, len(parts)),
        info, (4,),
        [tiles, tiles]
        + [whole(a) for a in parts]
        + [first, second, first, second],
        [whole(outs[0]), pl.BlockSpec((2, tile, columns), lambda i, s: (0, i, 0)), tiles, tiles],
        outs, (near, far, *parts, cosine, cosine, sine, sine),
        "project", 4 * rows * width * columns,
    )
    return out.reshape(2 * rows, columns), weight, act_near, act_far


def place_of(block):
    return (block & 1) | ((block >> 1) & 1) << 2 | ((block >> 2) & 1) << 1


def lowest_key(block, rows, bound):
    pos = block * rows + lax.broadcasted_iota(jnp.int32, (rows, 1), 0)
    return jnp.maximum(jnp.where(pos >= bound, bound, 0), pos - (WINDOW - 1))


def block_scores(query, key, low, q_block, k_block, rows):
    scores = dot_nt(query, key) * HD**-0.5
    pos = k_block * rows + lax.broadcasted_iota(jnp.int32, (rows, rows), 1)
    seen = pos >= low
    if q_block == k_block:
        seen = seen & (
            lax.broadcasted_iota(jnp.int32, (rows, rows), 1)
            <= lax.broadcasted_iota(jnp.int32, (rows, rows), 0)
        )
    return jnp.where(seen, scores, NEG)


def key_blocks(q_block, rows):
    return range(max(0, q_block - WINDOW // rows), q_block + 1)


def row_start(block, rank, rows):
    return pl.multiple_of(jnp.bitwise_xor(place_of(block), rank) * rows, rows)


def attend_kernel(info, qkv, *refs):
    near, far, lse, result = refs
    rows = qkv.shape[0] // 8
    rank, bound = info[RANK], info[BOUND]
    for b in range(8):
        own = pl.ds(row_start(b, rank, rows), rows)
        query = qkv[own, :HD]
        low = lowest_key(b, rows, bound)
        spots = [(kb, pl.ds(row_start(kb, rank, rows), rows)) for kb in key_blocks(b, rows)]
        scores = [
            block_scores(query, qkv[at, HD : 2 * HD], low, b, kb, rows) for kb, at in spots
        ]
        top = functools.reduce(jnp.maximum, [jnp.max(s, axis=1, keepdims=True) for s in scores])
        powered = [jnp.exp(s - top) for s in scores]
        total = functools.reduce(jnp.add, [jnp.sum(p, axis=1, keepdims=True) for p in powered])
        inverse = 1.0 / total
        out = functools.reduce(
            jnp.add,
            [
                dot((p * inverse).astype(BF16), qkv[at, 2 * HD :])
                for p, (_, at) in zip(powered, spots)
            ],
        )
        result[own, :] = out.astype(BF16)
        lse[0, own, :] = top + jnp.log(total)
    near[...] = result[: 4 * rows, :]
    far[...] = result[4 * rows :, :]


def attend(info, qkv):
    length = qkv.shape[0]
    rows = length // 8
    heads = qkv.shape[1] // (3 * HD)
    outs = [shape((4 * rows, heads * HD), BF16)] * 2 + [shape((heads, length, 1), F32)]
    return call(
        attend_kernel,
        info, (heads,), [pl.BlockSpec((length, 3 * HD), lambda h, s: (0, h))],
        [pl.BlockSpec((4 * rows, HD), lambda h, s: (0, h))] * 2
        + [pl.BlockSpec((1, length, 1), lambda h, s: (h, 0, 0))],
        outs, (qkv,), "attend", 8 * heads * length * WINDOW * HD,
        [pltpu.VMEM((length, HD), BF16)],
    )


def attend_back_kernel(info, qkv, *refs):
    grads, (lse, cosine, sine, out, top_all, sum_key, sum_value) = refs[:4], refs[4:]
    rows = qkv.shape[0] // 8
    rank, bound = info[RANK], info[BOUND]
    sum_key[...] = jnp.zeros_like(sum_key)
    sum_value[...] = jnp.zeros_like(sum_value)
    for j in range(4):
        top_all[j * rows : (j + 1) * rows, :] = grads[j][:rows, :]
        top_all[(j + 4) * rows : (j + 5) * rows, :] = grads[j][rows:, :]

    def unturn(value, at):
        value = value.astype(BF16).astype(F32)
        turned = value * cosine[at, :] - pltpu.roll(value, HD // 2, 1) * sine[at, :]
        return turned.astype(BF16)

    for b in range(8):
        own = pl.ds(row_start(b, rank, rows), rows)
        query = qkv[own, :HD]
        top = top_all[own, :]
        low = lowest_key(b, rows, bound)
        log_total = lse[0, own, :]
        spots = [(kb, pl.ds(row_start(kb, rank, rows), rows)) for kb in key_blocks(b, rows)]
        probs = [
            jnp.exp(block_scores(query, qkv[at, HD : 2 * HD], low, b, kb, rows) - log_total)
            for kb, at in spots
        ]
        slopes = [dot_nt(top, qkv[at, 2 * HD :]) for _, at in spots]
        mean = functools.reduce(
            jnp.add, [jnp.sum(p * g, axis=1, keepdims=True) for p, g in zip(probs, slopes)]
        )
        sum_query = jnp.zeros((rows, HD), F32)
        for p, g, (_, at) in zip(probs, slopes, spots):
            low_grad = (p * (g - mean)).astype(BF16)
            sum_query = sum_query + dot(low_grad, qkv[at, HD : 2 * HD])
            sum_key[at, :] += dot_tn(low_grad, query)
            sum_value[at, :] += dot_tn(p.astype(BF16), top)
        out[own, :HD] = unturn(sum_query * HD**-0.5, own)

    @pl.loop(0, 8)
    def _(j):
        at = pl.ds(pl.multiple_of(j * rows, rows), rows)
        out[at, HD : 2 * HD] = unturn(sum_key[at, :] * HD**-0.5, at)
        out[at, 2 * HD :] = sum_value[at, :].astype(BF16)


def attend_back(info, qkv, grads, lse, cosine, sine, head):
    length = qkv.shape[0]
    rows = length // 8
    out = shape((length, 3 * HD), BF16)
    return call(
        attend_back_kernel,
        info, (1,),
        [pl.BlockSpec((length, 3 * HD), lambda i, s: (0, head))]
        + [pl.BlockSpec((2 * rows, HD), lambda i, s: (0, head))] * 4
        + [pl.BlockSpec((1, length, 1), lambda i, s: (head, 0, 0))]
        + [whole(cosine), whole(sine)],
        whole(out), out, (qkv, *grads, lse, cosine, sine), "attend_back",
        20 * length * WINDOW * HD,
        [
            pltpu.VMEM((length, HD), BF16),
            pltpu.VMEM((length, HD), F32),
            pltpu.VMEM((length, HD), F32),
        ],
    )


def branch_kernel(piece, info, *refs):
    blocks = refs[:4]
    weight, tokens, attn, middle, scale, act = refs[4:]
    step = pl.program_id(0)
    width = weight.shape[1]

    @pl.when(step == 0)
    def _():
        rows = tokens.shape[0]
        for j in range(8):
            start = pl.multiple_of(jnp.bitwise_xor(info[RANK], j) * piece, piece)
            first = j // 4 * rows
            attn[:, pl.ds(start, piece)] = blocks[j % 4][first : first + rows, :]

    at = pl.ds(pl.multiple_of(step * width, width), width)
    middle[:, at] = tokens[:, at].astype(F32) + dot(attn[...], weight[...])

    @pl.when(step == pl.num_programs(0) - 1)
    def _():
        value = middle[...]
        inverse = lax.rsqrt(jnp.mean(value * value, axis=1, keepdims=True) + EPS)
        scale[...] = inverse
        act[...] = (value * inverse).astype(BF16)


def branch(info, blocks, weight, tokens):
    rows, width = tokens.shape
    outs = [
        shape((rows, width), BF16),
        shape((rows, width), F32),
        shape((rows, 1), F32),
        shape((rows, width), BF16),
    ]
    return call(
        functools.partial(branch_kernel, width // 8),
        info, (4,),
        [whole(a) for a in blocks]
        + [pl.BlockSpec((width, width // 4), lambda i, s: (0, i)), whole(tokens)],
        [whole(a) for a in outs], outs, (*blocks, weight, tokens), "branch",
        2 * rows * width * width,
    )


def slopes_kernel(info, near, far, first, second, out_near, out_far):
    columns = first.shape[0]
    for top, out in ((near, out_near), (far, out_far)):
        out[:, :columns] = dot_nt(top[...], first[...])
        out[:, columns:] = dot_nt(top[...], second[...])


def slopes(info, near, far, first, second):
    rows, width = near.shape
    tile = rows // 4
    columns = first.shape[0] + second.shape[0]
    tiles = pl.BlockSpec((tile, width), lambda i, s: (i, 0))
    return call(
        slopes_kernel,
        info, (4,), [tiles, tiles, whole(first), whole(second)],
        [pl.BlockSpec((tile, columns), lambda i, s: (i, 0))] * 2,
        [shape((rows, columns), F32)] * 2, (near, far, first, second), "slopes",
        4 * rows * width * columns,
    )


def ffn_kernel(tail, more, info, *refs):
    if more:
        act, slope, pair, earlier, earlier_pair, hidden, grads, back = refs
    else:
        act, slope, pair, hidden, grads = refs
    double = pair.shape[1]
    main = double // 2 - tail
    proj = dot(act[...], pair[...])

    def gated(gate, up, grad):
        sigmoid = jax.nn.sigmoid(gate)
        silu = gate * sigmoid
        return (
            silu * up,
            grad * up * sigmoid * (1.0 + gate * (1.0 - sigmoid)),
            grad * silu,
        )

    value, to_gate, to_up = gated(proj[:, :main], proj[:, double - main :], slope[:, :main])
    hidden[:, :main] = value.astype(BF16)
    grads[:, :main] = to_gate.astype(BF16)
    grads[:, double - main :] = to_up.astype(BF16)
    if tail:
        mixed = proj[:, main : main + 2 * tail]
        value, to_gate, to_up = gated(
            mixed, pltpu.roll(mixed, tail, 1), slope[:, main : main + 2 * tail]
        )
        first = lax.broadcasted_iota(jnp.int32, mixed.shape, 1) < tail
        hidden[:, main : main + 2 * tail] = jnp.where(first, value, 0.0).astype(BF16)
        grads[:, main : main + 2 * tail] = jnp.where(
            first, to_gate, pltpu.roll(to_up, tail, 1)
        ).astype(BF16)
    if more:
        total = dot_nt(grads[...], pair[...]) + dot_nt(earlier[...], earlier_pair[...])
        back[...] = total.astype(BF16)


def ffn(info, act, slope, chunk, pair, earlier=None, earlier_pair=None):
    rows, width = act.shape
    tile = rows // 4
    double = pair.shape[1]
    columns = -(-double // 256) * 128
    offset = slope.shape[1] // columns - 1 if chunk else 0
    more = earlier is not None
    tiles = pl.BlockSpec((tile, width), lambda i, s: (i, 0))
    operands = [act, slope, pair]
    in_specs = [tiles, pl.BlockSpec((tile, columns), lambda i, s: (i, offset)), whole(pair)]
    outs = [shape((rows, columns), BF16), shape((rows, double), BF16)]
    out_specs = [
        pl.BlockSpec((tile, columns), lambda i, s: (i, 0)),
        pl.BlockSpec((tile, double), lambda i, s: (i, 0)),
    ]
    flops = 2 * rows * width * double
    if more:
        operands += [earlier, earlier_pair]
        in_specs += [
            pl.BlockSpec((tile, earlier.shape[1]), lambda i, s: (i, 0)),
            whole(earlier_pair),
        ]
        outs += [shape((rows, width), BF16)]
        out_specs += [tiles]
        flops += 2 * rows * width * (double + earlier.shape[1])
    return call(
        functools.partial(ffn_kernel, double // 2 % 128, more),
        info, (4,), in_specs, out_specs, outs, operands, "ffn", flops,
    )


def grad_rows_kernel(own_rows, info, act_near, act_far, near, far, *refs):
    outs, total = refs[:-1], refs[-1]
    total[...] = dot_tn(act_near[...], near[...]) + dot_tn(act_far[...], far[...])
    for i, out in enumerate(outs):

        @pl.when(pl.program_id(0) == i)
        def _():
            for k in range(4):
                start = jnp.bitwise_xor(info[SHARD], k) * own_rows
                value = total[pl.ds(pl.multiple_of(start, own_rows), own_rows), :]
                out[k * own_rows : (k + 1) * own_rows, :] = value.astype(BF16)


def grad_rows(info, act_near, act_far, near, far, count, name, split=False):
    rows, width = act_near.shape
    chunk = width // count
    columns = near.shape[1]

    def spot(i, s):
        return (0, s[PLANES + (i + 1) % count])

    acts = pl.BlockSpec((rows, chunk), spot)
    outs = [shape((chunk, columns), BF16)] * count
    first = pl.BlockSpec((rows, columns), lambda i, s: (0, 0))
    second = pl.BlockSpec((rows, columns), lambda i, s: (1 if split else 0, 0))
    return call(
        functools.partial(grad_rows_kernel, chunk // 4),
        info, (count,), [acts, acts, first, second], [whole(a) for a in outs], outs,
        (act_near, act_far, near, far), name, 4 * rows * width * columns,
        [pltpu.VMEM((chunk, columns), F32)],
    )


def grad_down_kernel(rows, info, first_near, first_far, second_near, second_far, *refs):
    top_near, top_far = refs[:2]
    outs, total = refs[2:-1], refs[-1]
    count = len(outs)
    start = 0
    for near, far, part in ((first_near, first_far, rows[0]), (second_near, second_far, rows[1])):
        units = near.shape[1]
        total[:units, :] = dot_tn(near[...], top_near[...]) + dot_tn(far[...], top_far[...])
        for i in range(count):
            at = pl.multiple_of(info[PLANES + (i + 1) % count] * part, part)
            outs[i][start : start + part, :] = total[pl.ds(at, part), :].astype(BF16)
        start += part


def grad_down(info, first, second, top_near, top_far, count, rows):
    tokens, width = top_near.shape
    part = width // 4
    outs = [shape((sum(rows), width), BF16)] * count
    tops = pl.BlockSpec((tokens, part), lambda i, s: (0, i))
    hidden = (*first, *second)
    units = max(a.shape[1] for a in hidden)
    return call(
        functools.partial(grad_down_kernel, rows),
        info, (4,), [whole(a) for a in hidden] + [tops, tops],
        [pl.BlockSpec((sum(rows), part), lambda i, s: (0, i))] * count, outs,
        (*hidden, top_near, top_far), "grad_down",
        4 * tokens * width * (first[0].shape[1] + second[0].shape[1]),
        [pltpu.VMEM((units, part), F32)],
    )


def matmul_two_kernel(info, a, b, c, d, out):
    out[...] = (dot(a[...], b[...]) + dot(c[...], d[...])).astype(BF16)


def down_product(info, first, second, down_first, down_second):
    rows, width = first.shape[0], down_first.shape[1]
    tile = rows // 4
    out = shape((rows, width), BF16)
    return call(
        matmul_two_kernel,
        info, (4,),
        [
            pl.BlockSpec((tile, first.shape[1]), lambda i, s: (i, 0)), whole(down_first),
            pl.BlockSpec((tile, second.shape[1]), lambda i, s: (i, 0)), whole(down_second),
        ],
        pl.BlockSpec((tile, width), lambda i, s: (i, 0)), out,
        (first, down_first, second, down_second), "down_product",
        2 * rows * width * (first.shape[1] + second.shape[1]),
    )


def grad_attn_kernel(info, *refs):
    own, first, second, third, top, middle, scale, weight = refs[:8]
    grad_middle, branch_ref, near, far = refs[8:]
    step = pl.program_id(0)
    rows = own.shape[0]

    @pl.when(step == 0)
    def _():
        grad = own[...]
        for moved in (first, second, third):
            grad = grad + moved[...].astype(F32)
        value, inverse = middle[...], scale[...]
        mean = jnp.mean(grad * value, axis=1, keepdims=True)
        total = top[...].astype(F32) + inverse * grad - value * (inverse**3 * mean)
        grad_middle[...] = total
        branch_ref[...] = total.astype(BF16)

    value = dot_nt(branch_ref[...], weight[...]).astype(BF16)
    for j in range(8):

        @pl.when(step == j)
        def _():
            out = far if j > 3 else near
            out[j % 4 * rows : (j % 4 + 1) * rows, :] = value


def grad_attn(info, own, parts, top, middle, scale, weight):
    rows, width = middle.shape
    piece = width // 8
    outs = [shape((rows, width), F32), shape((rows, width), BF16)]
    outs += [shape((4 * rows, piece), BF16)] * 2
    operands = (own, *parts, top, middle, scale)

    def spot(i, s):
        return (jnp.bitwise_xor(s[RANK], i), 0)

    return call(
        grad_attn_kernel,
        info, (8,), [whole(a) for a in operands] + [pl.BlockSpec((piece, width), spot)],
        [whole(a) for a in outs], outs, (*operands, weight), "grad_attn",
        2 * rows * width * width,
    )


def grad_out_kernel(info, attn, near_cols, far_cols, near, far):
    near[0] = dot_tn(attn[...], near_cols[...]).astype(BF16)
    far[0] = dot_tn(attn[...], far_cols[...]).astype(BF16)


def grad_out_terms(info, attn, grad):
    rows, width = attn.shape
    piece = width // 8
    outs = [shape((4, width, piece), BF16)] * 2
    return call(
        grad_out_kernel,
        info, (4,),
        [
            whole(attn),
            pl.BlockSpec((rows, piece), lambda i, s: (0, jnp.bitwise_xor(s[RANK], i))),
            pl.BlockSpec((rows, piece), lambda i, s: (0, jnp.bitwise_xor(s[RANK], i + 4))),
        ],
        [pl.BlockSpec((1, width, piece), lambda i, s: (i, 0, 0))] * 2, outs,
        (attn, grad, grad), "grad_out", 2 * rows * width * width,
    )


def order_kernel(own_rows, info, own, first, second, third, *refs):
    outs, total = refs[:-1], refs[-1]
    count = len(outs)
    value = own[...]
    for moved in (first, second, third):
        value = value + moved[...].astype(F32)
    total[...] = value
    for i, out in enumerate(outs):
        for k in range(4):
            block = info[PLANES + (i + 1) % count] * 4 + jnp.bitwise_xor(info[SHARD], k)
            value = total[pl.ds(pl.multiple_of(block * own_rows, own_rows), own_rows), :]
            out[k * own_rows : (k + 1) * own_rows, :] = value.astype(BF16)


def order_out(info, own, parts, count):
    width, columns = own.shape
    outs = [shape((width // count, columns), BF16)] * count
    return call(
        functools.partial(order_kernel, width // count // 4),
        info, (1,), [whole(a) for a in (own, *parts)], [whole(a) for a in outs], outs,
        (own, *parts), "order_out", 0, [pltpu.VMEM((width, columns), F32)],
    )


def back_product_kernel(info, first, second, weight, out):
    columns = first.shape[1]
    total = dot_nt(first[...], weight[:, :columns]) + dot_nt(second[...], weight[:, columns:])
    out[...] = total.astype(BF16)


def back_product(info, first, second, weight, far):
    rows, width = first.shape[0] // 2, weight.shape[0]
    tile = rows // 4
    out = shape((rows, width), BF16)
    tiles = pl.BlockSpec((tile, first.shape[1]), lambda i, s: (i + (4 if far else 0), 0))
    return call(
        back_product_kernel,
        info, (4,), [tiles, tiles, whole(weight)],
        pl.BlockSpec((tile, width), lambda i, s: (i, 0)), out, (first, second, weight),
        "back_product", 2 * rows * width * weight.shape[1],
    )


def rank_block(info, j, mine, theirs):
    rows = mine.shape[0] // 4
    source = theirs if j % 2 else mine
    return source[j // 2 * rows : (j // 2 + 1) * rows, :]


def finish_qkv_kernel(info, *refs):
    pairs = (refs[:2], refs[2:4])
    weight, gain, out, gain_out = refs[4:]
    rows, width = out.shape[0], out.shape[1] // 3
    total = jnp.zeros((rows, HD), F32)
    for j in range(8):
        rank = jnp.bitwise_xor(info[RANK], j)
        for head, pair in enumerate(pairs):
            block = rank_block(info, j, *pair)
            for part in range(3):
                start = pl.multiple_of(part * width + (2 * rank + head) * HD, HD)
                value = block[:, part * HD : (part + 1) * HD].astype(F32)
                out[:, pl.ds(start, HD)] = value * gain[...]
                total = total + value * weight[:, pl.ds(start, HD)].astype(F32)
    gain_out[...] = jnp.sum(total, axis=1, keepdims=True)


def finish_qkv(info, first, second, weight, gain):
    outs = [shape(weight.shape, F32), shape(gain.shape, F32)]
    operands = (*first, *second, weight, gain)
    return call(
        finish_qkv_kernel,
        info, (1,), [whole(a) for a in operands], [whole(a) for a in outs], outs, operands,
        "finish_qkv", 0,
    )


def finish_out_kernel(info, mine, theirs, out):
    piece = mine.shape[1]
    for j in range(8):
        start = pl.multiple_of(jnp.bitwise_xor(info[RANK], j) * piece, piece)
        out[:, pl.ds(start, piece)] = rank_block(info, j, mine, theirs).astype(F32)


def finish_out(info, mine, theirs):
    rows, piece = mine.shape[0] // 4, mine.shape[1]
    out = shape((rows, 8 * piece), F32)
    return call(
        finish_out_kernel,
        info, (1,), [whole(mine), whole(theirs)], whole(out), out, (mine, theirs),
        "finish_out", 0,
    )


def unit_lanes(first, count, local):
    main = local // 128 * 128
    runs = []
    while count:
        size = min(count, main - first) if first < main else count
        up = local + (local - main) + first if first < main else local + first - main
        runs.append((first, up, size))
        first, count = first + size, count - size
    return runs


def finish_pair_kernel(planes, reals, pads, info, *refs):
    chunks = (refs[:2], refs[2:4])
    weights, gain, outs, gain_out = refs[4:6], refs[6], refs[7:9], refs[9]
    held = refs[10:]
    rows, width = outs[0].shape
    half_down = sum(reals)
    for (mine, theirs), by_rank in zip(chunks, held):
        for j in range(8):
            start = jnp.bitwise_xor(info[RANK], j) * rows
            block = rank_block(info, j, mine, theirs)
            by_rank[pl.ds(pl.multiple_of(start, rows), rows), :] = block[...].astype(F32)

    def move(chunk, rank, lane, out, column, size):
        source, target = lane // 128 * 128, column // 128 * 128
        wide = 128 if (lane - source) + size <= 128 and (column - target) + size <= 128 else 256
        at = slice(rank * rows, (rank + 1) * rows)
        if (lane - source) + size <= 128:
            value = held[chunk][at, source : source + 128]
            if wide == 256:
                value = jnp.concatenate([value, value], axis=1)
        else:
            value = held[chunk][at, source : source + 256]
        shift = ((column - target) - (lane - source)) % wide
        if shift:
            value = pltpu.roll(value, shift, 1)
        lanes = lax.broadcasted_iota(jnp.int32, value.shape, 1)
        keep = (lanes >= column - target) & (lanes < column - target + size)
        spot = slice(target, min(target + wide, width))
        if target + wide > width:
            value, keep = value[:, : width - target], keep[:, : width - target]
        out[:, spot] = jnp.where(keep, value, out[:, spot])

    for plane in range(planes):
        for rank in range(8):
            shard = 2 * (rank >> 1 & 1) + (rank >> 2)
            column = ((plane * 4 + shard) * 2 + (rank & 1)) * half_down
            for chunk, (real, pad) in enumerate(zip(reals, pads)):
                start = column
                for gate, up, size in unit_lanes(plane * pad, real, planes * pad):
                    move(chunk, rank, gate, outs[0], start, size)
                    move(chunk, rank, up, outs[1], start, size)
                    start += size
                column += real
    total = jnp.zeros((rows, 128), F32)
    for weight, out in zip(weights, outs):
        for tile in range(width // 128):
            at = slice(tile * 128, (tile + 1) * 128)
            value = out[:, at]
            total = total + value * weight[:, at].astype(F32)
            out[:, at] = value * gain[...]
    gain_out[...] = jnp.sum(total, axis=1, keepdims=True)


def finish_pair(info, first, second, gate, up, gain, planes, reals, pads):
    rows = gate.shape[0]
    outs = [shape(gate.shape, F32)] * 2 + [shape(gain.shape, F32)]
    operands = (*first, *second, gate, up, gain)
    return call(
        functools.partial(finish_pair_kernel, planes, reals, pads),
        info, (1,), [whole(a) for a in operands], [whole(a) for a in outs], outs, operands,
        "finish_pair", 0,
        [pltpu.VMEM((8 * rows, pair[0].shape[1]), F32) for pair in (first, second)],
    )


def on_device(
    planes,
    tokens,
    bounds,
    norm_attn,
    weight_qkv,
    weight_out,
    norm_ffn,
    weight_gate,
    weight_up,
    weight_down,
    cotangent,
):
    rows, width = tokens.shape[1], tokens.shape[2]
    own_rows = weight_qkv.shape[0]
    half_down = weight_down.shape[0] // 2
    cut = -(-half_down // 32) * 16
    pads = (cut, -(-(half_down - cut) // 16) * 16)
    reals = (cut, half_down - cut)
    starts = (0, cut)

    y, z, x, c = (lax.axis_index(name) for name in ("y", "z", "x", "c"))
    rank = 4 * c + 2 * x + y
    shard = 2 * x + c
    ring_list = ring_of(planes)
    table = [
        [ring_list[(ring_list.index(i) - s) % planes] for s in range(planes)]
        for i in range(planes)
    ]
    arrival = jnp.asarray(table, jnp.int32)[z]
    boundary = lax.dynamic_index_in_dim(bounds, z, 0, False)
    info = jnp.concatenate([jnp.stack([rank, boundary, shard]).astype(jnp.int32), arrival])
    order = Order()
    do, need = order.do, order.need
    lane_a, lane_b = Lane(planes), Lane(planes)

    def spread_pieces(pieces):
        return [hop(piece, j) for piece, j in zip(pieces, SHARD_TO_RANK)]

    def owners(total):
        return [
            hop(total[k * own_rows : (k + 1) * own_rows], SHARD_TO_RANK[k]) for k in (2, 1, 3)
        ]

    def rows_of(total, pieces):
        need(*pieces)
        mine = do(join, info, (total, 0, own_rows), *pieces)
        return mine, hop(mine, 1)

    down_own = lax.dynamic_slice_in_dim(weight_down, y * half_down, half_down, 0)
    down_own = jnp.pad(down_own, [(0, sum(pads) - half_down), (0, 0)])
    down_got = lane_a.gather(down_own, 1)
    wide_attn = norm_attn.astype(F32)[:, None]
    wide_ffn = norm_ffn.astype(F32)[:, None]
    pieces = spread_pieces(do(pack, info, weight_qkv, weight_out, wide_attn))
    token_parts = near_parts(tokens[0], (), pieces[1:])

    def split_hidden(weight):
        split = (after(weight, *pieces).astype(F32) * wide_ffn).astype(BF16)
        split = split.reshape(own_rows, planes, 2, 2, 2, half_down)
        return split.transpose(3, 2, 4, 0, 1, 5).reshape(8, own_rows, planes, half_down)

    gate_split, up_split = split_hidden(weight_gate), split_hidden(weight_up)
    pair_pieces = []
    for start, real, pad in zip(starts, reals, pads):
        both = []
        for split in (gate_split, up_split):
            part = split[..., start : start + real]
            part = jnp.pad(part, [(0, 0)] * 3 + [(0, pad - real)])
            both.append(part.reshape(8, own_rows, planes * pad))
        main = planes * pad // 128 * 128
        pair_pieces += [both[0], both[1][..., main:], both[1][..., :main]]
    pair_pieces = jnp.concatenate(pair_pieces, axis=-1)
    pair_pieces = spread_pieces(
        [
            lax.dynamic_index_in_dim(pair_pieces, jnp.bitwise_xor(rank, j), 0, False)
            for j in SHARD_TO_RANK
        ]
    )

    blocks = jnp.asarray([place_of(i) for i in range(8)], jnp.int32)
    blocks = jnp.take(blocks, jnp.bitwise_xor(jnp.arange(8, dtype=jnp.int32), rank))
    positions = (blocks[:, None] * rows + jnp.arange(rows, dtype=jnp.int32)[None, :]).reshape(-1)
    frequency = THETA ** (-jnp.arange(HD // 2, dtype=F32) * 2.0 / HD)
    angles = positions.astype(F32)[:, None] * frequency[None, :]
    cosine = jnp.cos(angles)
    sine = jnp.sin(angles)
    cosine = jnp.concatenate([cosine, cosine], axis=1)
    sine = jnp.concatenate([-sine, sine], axis=1)

    need(down_got[1], *pieces[1:])
    qkv_plane, out_plane = do(join_two, info, 3 * (width // 8), *pieces)
    out_got = lane_b.gather(out_plane)
    qkv_got = lane_b.gather(qkv_plane)
    need(*out_got)
    out_cols = do(join, info, *out_got)
    need(qkv_got[1], *pair_pieces[1:])
    pair_first, pair_second = do(join_two, info, 2 * planes * pads[0], *pair_pieces)
    out_parts = near_parts(out_cols, token_parts[1:2], pair_pieces, token_parts)
    need(*token_parts, qkv_got[2])
    tokens_near = do(join, info, *token_parts)
    tokens_far = hop(tokens_near, 4)
    lane_a.last = (qkv_got[-1],)
    pair_first_got = lane_b.gather(pair_first)
    down_got = lane_a.gather(down_got)
    pair_second_got = lane_a.gather(pair_second)
    need(tokens_far, *qkv_got)
    qkv, full_qkv, act_near, act_far = do(
        project, info, tokens_near, tokens_far, qkv_got, cosine, sine
    )
    need(*out_parts, down_got[2], pair_first_got[1])
    out_near = do(join, info, *out_parts)
    out_far = hop(out_near, 4)
    top_parts = near_parts(after(cotangent[0], *out_parts))
    attn_near, attn_far, lse = do(attend, info, qkv)
    moved = hop(attn_far, 4)
    need(out_far)
    full_out = do(spread, info, out_near, out_far, planes)
    need(moved, pair_first_got[2])
    attn_moved = near_moves(do(meet, info, attn_near, moved))
    need(*attn_moved)
    attn, middle, scale, act_own = do(branch, info, attn_moved, full_out, tokens[0])
    act_parts = near_parts(act_own)
    need(*top_parts, *down_got)
    top_near = do(join, info, *top_parts)
    top_far = hop(top_near, 4)
    need(*pair_first_got)
    down_a, down_b = do(stack_planes, info, pads[0], *down_got)
    need(top_far)
    slope_near, slope_far = do(slopes, info, top_near, top_far, down_a, down_b)
    full_first = do(assemble, info, *pair_first_got)
    need(*act_parts, pair_second_got[1])
    ffn_near = do(join, info, *act_parts)
    ffn_far = hop(ffn_near, 4)

    hidden_near, grads_near = do(ffn, info, ffn_near, slope_near, 0, full_first)
    need(ffn_far, pair_second_got[2])
    hidden_far, grads_far = do(ffn, info, ffn_far, slope_far, 0, full_first)
    lane_c = Lane(planes)
    pair_a = Sum(
        order,
        lane_b,
        do(grad_rows, info, ffn_near, ffn_far, grads_near, grads_far, planes, "grad_pair"),
    )
    need(*pair_second_got)
    full_second = do(assemble, info, *pair_second_got)
    second_far, more_far, far_terms = do(
        ffn, info, ffn_far, slope_far, 1, full_second, grads_far, full_first
    )
    moved = hop(far_terms, 4)
    second_near, more_near, near_terms = do(
        ffn, info, ffn_near, slope_near, 1, full_second, grads_near, full_first
    )
    pair_a.move()
    need(moved)
    own, parts = scatter_moves(*do(combine, info, near_terms, moved))
    pair_b = Sum(
        order,
        lane_a,
        do(grad_rows, info, ffn_near, ffn_far, more_near, more_far, planes, "grad_pair"),
    )
    pair_a.move()
    down_sum = Sum(
        order,
        lane_b,
        do(
            grad_down, info, (hidden_near, hidden_far), (second_near, second_far),
            top_near, top_far, planes, pads,
        ),
    )
    block_near = do(down_product, info, hidden_near, second_near, down_a, down_b)
    need(*parts)

    grad_middle, grad_branch, attn_near, attn_far = do(
        grad_attn, info, own, parts, cotangent[0], middle, scale, full_out
    )
    pair_a.move()
    away = hop(attn_far, 4)
    near_out, far_out = do(grad_out_terms, info, attn, grad_branch)
    pair_b.move()
    first_pieces = owners(pair_a.total)
    need(away)
    attn_grads = near_moves(do(meet, info, attn_near, away))
    out_moved = hop(after(far_out, attn_grads[0]), 4)
    need(*first_pieces)
    block_far = do(down_product, info, hidden_far, second_far, down_a, down_b)
    need(*attn_grads)
    grads_first = do(attend_back, info, qkv, attn_grads, lse, cosine, sine, 0)
    pair_b.move()
    sums_first = rows_of(pair_a.total, first_pieces)
    need(out_moved)
    out_own, out_parts = scatter_moves(*do(combine, info, near_out, out_moved))
    down_sum.move()
    qkv_first = Sum(
        order,
        lane_a,
        do(grad_rows, info, act_near, act_far, grads_first, grads_first, planes, "grad_qkv", True),
    )
    block_moved = hop(after(block_far, qkv_first.total), 4)
    grads_second = do(attend_back, info, qkv, attn_grads, lse, cosine, sine, 1)
    pair_b.move()
    second_pieces = owners(after(pair_b.total, *out_parts))
    need(block_moved)
    block_terms = do(combine, info, block_near, block_moved)
    qkv_first.move()
    need(*out_parts)
    qkv_second = Sum(
        order,
        lane_b,
        do(
            grad_rows, info, act_near, act_far, grads_second, grads_second, planes,
            "grad_qkv", True,
        ),
    )
    block_own, block_parts = scatter_moves(block_terms[0], *after(block_terms[1:], *out_parts))
    down_sum.move()

    in_far = do(back_product, info, grads_first, grads_second, full_qkv, True)
    in_moved = hop(in_far, 4)
    qkv_first.move()
    in_near = do(back_product, info, grads_first, grads_second, full_qkv, False)
    out_sum = Sum(order, lane_c, do(order_out, info, out_own, out_parts, planes))
    sums_second = rows_of(pair_b.total, second_pieces)
    down_sum.move()
    qkv_second.move()
    need(in_moved)
    in_own, in_parts = scatter_moves(*do(combine, info, in_near, in_moved))
    qkv_first.move()
    out_sum.move()
    down_mine = down_sum.total[:half_down]
    down_theirs = hop(down_mine, 1)
    need(*sums_first, *sums_second, *block_parts)
    sum_gate, sum_up, gain_sum_ffn = do(
        finish_pair, info, sums_first, sums_second, weight_gate, weight_up, wide_ffn,
        planes, reals, pads,
    )
    first_pieces = owners(qkv_first.total)
    qkv_second.move()
    out_sum.finish()
    need(*in_parts)
    first_rows = rows_of(qkv_first.total, first_pieces)
    out_pieces = owners(out_sum.total)
    qkv_second.finish()
    second_pieces = owners(qkv_second.total)
    out_rows = rows_of(out_sum.total, out_pieces)
    second_rows = rows_of(qkv_second.total, second_pieces)

    down_both = jnp.stack([down_mine, down_theirs])
    sum_down = jnp.concatenate(
        [lax.dynamic_index_in_dim(down_both, jnp.bitwise_xor(y, i), 0, False) for i in range(2)]
    ).astype(F32)
    need(out_rows[1])
    sum_out = do(finish_out, info, *out_rows)
    need(first_rows[1], second_rows[1])
    sum_qkv, gain_sum_attn = do(
        finish_qkv, info, first_rows, second_rows, weight_qkv, wide_attn
    )
    block_out = middle + block_own + sum(part.astype(F32) for part in block_parts)
    inputs = tokens[0].astype(F32)
    inv_attn = lax.rsqrt(jnp.mean(inputs * inputs, axis=-1, keepdims=True) + EPS)
    scaled = in_own + sum(part.astype(F32) for part in in_parts)
    grad_tokens = (
        grad_middle
        + inv_attn * scaled
        - inputs * inv_attn**3 * jnp.mean(scaled * inputs, axis=-1, keepdims=True)
    )
    return (
        block_out.astype(BF16)[None],
        grad_tokens[None],
        gain_sum_attn[:, 0],
        sum_qkv,
        sum_out,
        gain_sum_ffn[:, 0],
        sum_gate,
        sum_up,
        sum_down,
    )


def solution(mesh):
    planes = mesh.shape["fsdp"] // 4
    grid = Mesh(mesh.devices.reshape(2, planes, 2, 2), ("y", "z", "x", "c"))
    fsdp = ("z", "x", "c")
    by_token = P(fsdp, "y", None)
    by_row = P(fsdp, None)
    gain = P(fsdp)
    return jax.shard_map(
        functools.partial(on_device, planes),
        mesh=grid,
        in_specs=(
            by_token, P(), gain, by_row, by_row, gain, by_row, by_row, by_row, by_token,
        ),
        out_specs=(
            by_token, by_token, gain, by_row, by_row, gain, by_row, by_row, by_row,
        ),
        check_vma=False,
    )
```
